32 devices in a mesh: chan: 4 (over y, x), tm: 8 (over z, core).
Axes of the slice: x: 2, y: 2, z: 4, core: 2. Of those that a mesh axis runs over, the one named last changes fastest.
Arguments:
- records: bfloat16 [8, 1536, 1536], P('tm', 'chan')
- partners: int32 [4, 3], P('chan'), may hold values from 0 to 3, as said below
- counts: int32 [4], P('chan'), may hold values from 1 to 3, as said below
- sources: int32 [4, 2], P('chan'), may hold values from 0 to 383, as said below
Outputs:
- xcorr: float32 [4, 384, 3, 2, 384], P('chan', 'tm')
The draws below stay inside these ranges and needn't reach their ends.
Inputs may be any that keep to these rules, and one draw needn't show every extreme that they name: `partners`: each row holds 3 different blocks. `counts`: some block has all 3 slots live. `sources`: each row holds 2 different channels.
All inputs are finite; a program needn't handle non-finite values.
Results may differ from the reference program's by a relative error of at most 0.008.
Values may be sent and summed in bfloat16 or wider, within the bound.
No kernel may reach another device: no remote copies, remote signals or barrier semaphores. Data moves between devices by JAX's collectives and lax.ppermute only.
A program may use at most 64 MiB of HBM per device.

```python
import math
import jax
import jax.numpy as jnp
from jax import lax

CH = 384
L = 1536
F = 320
HL = 192
SMOOTH = 32
S = 2
P_SIZE = 3
NB = 4
NW = 8


def draw_records(key, part):
    keys = jax.random.split(key, 6)
    channels = NB * CH
    noise = jax.random.normal(keys[0], (NW, channels, L), jnp.float32)
    chan_scale = jnp.exp(jax.random.uniform(keys[1], (1, channels, 1), jnp.float32, 0.0, math.log(10.0)))
    win_scale = jnp.exp(jax.random.uniform(keys[2], (NW, 1, 1), jnp.float32, math.log(0.5), math.log(2.0)))
    tone_bin = jax.random.randint(keys[3], (1, channels, 1), 1, F + 1)
    tone_phase = jax.random.uniform(keys[4], (NW, channels, 1), jnp.float32, -math.pi, math.pi)
    tone_size = jax.random.uniform(keys[5], (1, channels, 1), jnp.float32, 0.0, 4.0)
    sample_index = jnp.arange(L, dtype=jnp.int32)[None, None, :]
    angle = (tone_bin * sample_index % L).astype(jnp.float32) * (2.0 * math.pi / L) + tone_phase
    signal = chan_scale * win_scale * (noise + tone_size * jnp.sin(angle))
    return signal.astype(jnp.bfloat16)


def shifted_rows(key, rows, total, picked):
    keys = jax.random.split(key, 2)
    row_keys = jax.random.split(keys[0], rows)
    perms = jax.vmap(lambda one_key: jax.random.permutation(one_key, total)[:picked])(row_keys)
    chosen = jax.random.randint(keys[1], (), 0, rows)
    row_index = jnp.arange(rows, dtype=jnp.int32)
    target = jnp.where(row_index == chosen, total - 1, jnp.where(row_index == (chosen + 1) % rows, 0, perms[:, 0]))
    return jnp.mod(perms - perms[:, :1] + target[:, None], total).astype(jnp.int32)


def draw_partners(key, part):
    return shifted_rows(jax.random.fold_in(key, 5), NB, NB, P_SIZE)


def draw_counts(key, part):
    keys = jax.random.split(key, 2)
    values = jax.random.randint(keys[0], (NB,), 1, P_SIZE + 1)
    chosen = jax.random.randint(keys[1], (), 0, NB)
    values = values.at[(chosen + 1) % NB].set(1)
    return values.at[chosen].set(P_SIZE).astype(jnp.int32)


def draw_sources(key, part):
    return shifted_rows(jax.random.fold_in(key, 11), NB, CH, S)


def setup_inputs(seed: int = 0) -> dict:
    arg_keys = jax.random.split(jax.random.key(seed), 5)
    records = draw_records(jax.random.fold_in(arg_keys[4], 71), 0)
    partners = draw_partners(jax.random.fold_in(arg_keys[4], 71), 0)
    counts = draw_counts(jax.random.fold_in(arg_keys[4], 71), 0)
    sources = draw_sources(jax.random.fold_in(arg_keys[4], 71), 0)
    return {"records": records, "partners": partners, "counts": counts, "sources": sources}


def dft_table(length, bins):
    sample_index = jnp.arange(length, dtype=jnp.int32)[:, None]
    bin_index = jnp.arange(bins, dtype=jnp.int32)[None, :] + 1
    phase_index = sample_index * bin_index % length
    angle = phase_index.astype(jnp.float32) * (2.0 * math.pi / length)
    return jnp.concatenate([jnp.cos(angle), -jnp.sin(angle)], axis=1).astype(jnp.bfloat16)

def lag_table(length, bins, half):
    bin_index = jnp.arange(bins, dtype=jnp.int32)[:, None] + 1
    lag_index = jnp.arange(2 * half, dtype=jnp.int32)[None, :] - half
    phase_index = jnp.mod(bin_index * lag_index, length)
    angle = phase_index.astype(jnp.float32) * (2.0 * math.pi / length)
    return jnp.concatenate([jnp.cos(angle), -jnp.sin(angle)], axis=0)

def band_table(bins, half):
    input_bin = jnp.arange(bins, dtype=jnp.int32)[:, None]
    output_bin = jnp.arange(bins, dtype=jnp.int32)[None, :]
    centre = jnp.clip(output_bin, half, bins - 1 - half)
    return (jnp.abs(input_bin - centre) <= half).astype(jnp.float32)

def whiten(block_records):
    windows, channels, length = block_records.shape
    signal = block_records.astype(jnp.float32)
    signal = signal - lax.optimization_barrier(jnp.mean(signal, axis=-1, keepdims=True))
    demeaned = signal.astype(jnp.bfloat16).reshape(windows * channels, length)
    spectrum = jnp.dot(demeaned, dft_table(L, F), preferred_element_type=jnp.float32)
    real_part = spectrum[:, :F]
    imag_part = spectrum[:, F:]
    amplitude = jnp.sqrt(real_part * real_part + imag_part * imag_part)
    smooth = jnp.dot(amplitude, band_table(F, SMOOTH), precision=lax.Precision.HIGHEST) / (2 * SMOOTH + 1)
    factor = 1.0 / (smooth + 1e-06)
    whitened = jnp.concatenate([real_part * factor, imag_part * factor], axis=1)
    return whitened.astype(jnp.bfloat16).reshape(windows, channels, 2 * F)

def reference(records, partners, counts, sources):
    by_block = records.reshape(NW, NB, CH, L).transpose(1, 0, 2, 3)
    white = lax.map(whiten, by_block)
    inverse = lag_table(L, F, HL)
    scale = 1.0 / math.sqrt(F * NW)

    def one_block(block):
        own = white[block]
        source_spec = jnp.take(own, sources[block], axis=1).astype(jnp.float32)
        partner_spec = jnp.take(white, partners[block], axis=0).astype(jnp.float32)
        live = (jnp.arange(P_SIZE, dtype=jnp.int32) < counts[block]).astype(jnp.float32)
        src_real = source_spec[..., :F]
        src_imag = source_spec[..., F:]
        rec_real = partner_spec[..., :F]
        rec_imag = partner_spec[..., F:]
        cross_real = jnp.einsum('wsf,pwcf->cpsf', src_real, rec_real) + jnp.einsum('wsf,pwcf->cpsf', src_imag, rec_imag)
        cross_imag = jnp.einsum('wsf,pwcf->cpsf', src_real, rec_imag) - jnp.einsum('wsf,pwcf->cpsf', src_imag, rec_real)
        stacked = jnp.concatenate([cross_real, cross_imag], axis=-1) * live[None, :, None, None]
        lagged = jnp.dot(stacked.reshape(CH * P_SIZE * S, 2 * F), inverse, precision=lax.Precision.HIGHEST)
        return lagged.reshape(CH, P_SIZE, S, 2 * HL) * scale
    return lax.map(one_block, jnp.arange(NB, dtype=jnp.int32))
```

```python
import functools
import math

import jax
import jax.numpy as jnp
import ml_dtypes
import numpy as np
from jax import lax
from jax.experimental import pallas as pl
from jax.experimental.pallas import tpu as pltpu
from jax.sharding import PartitionSpec as P

L = 1536
F = 320
HL = 192
SMOOTH = 32
LANES = 128
MAIN = F // LANES * LANES
TAIL = F - MAIN
WIDTH = 2 * F
SRC_ROWS = 8
F32 = jnp.float32
BF16 = jnp.bfloat16


def dft_table():
    n = np.arange(L)[:, None]
    k = np.arange(F)[None, :] + 1
    angle = (n * k % L).astype(np.float32) * np.float32(2.0 * math.pi / L)
    c, s = np.cos(angle), -np.sin(angle)
    table = np.concatenate([c[:, :MAIN], s[:, :MAIN], c[:, MAIN:], s[:, MAIN:]], axis=1)
    return table.astype(ml_dtypes.bfloat16)


def band_table():
    bins = np.concatenate([np.arange(MAIN), np.arange(MAIN, F), np.arange(MAIN, F)])
    centre = np.clip(bins, SMOOTH, F - 1 - SMOOTH)
    band = np.abs(bins[:, None] - centre[None, :]) <= SMOOTH
    band[F:] = False
    return band.astype(ml_dtypes.bfloat16)


def lag_tables(scale):
    k = np.arange(F)[:, None] + 1
    j = np.arange(2 * HL)[None, :] - HL
    angle = np.mod(k * j, L).astype(np.float32) * np.float32(2.0 * math.pi / L)
    c, s = np.cos(angle) * np.float32(scale), -np.sin(angle) * np.float32(scale)
    table = np.concatenate([c[:MAIN], s[:MAIN], c[MAIN:], c[MAIN:], s[MAIN:], -s[MAIN:]], axis=0)
    high = table.astype(ml_dtypes.bfloat16)
    low = (table - high.astype(np.float32)).astype(ml_dtypes.bfloat16)
    return high, low


def whiten_kernel(chunks, shared, zs, src_ref, rec_ref, tab_ref, band_ref, *rest):
    outs, white = rest[:-1], rest[-1]
    rows = rec_ref.shape[0]
    signal = rec_ref[...].astype(F32)
    signal = signal - jnp.sum(signal, axis=1, keepdims=True) * (1.0 / L)
    spec = jnp.dot(signal.astype(BF16), tab_ref[...], preferred_element_type=F32)
    re, im, tail = spec[:, :MAIN], spec[:, MAIN : 2 * MAIN], spec[:, 2 * MAIN :]
    tail_sq = tail * tail
    amp = jnp.sqrt(
        jnp.concatenate([re * re + im * im, tail_sq + pltpu.roll(tail_sq, TAIL, 1)], axis=1)
    )
    high = amp.astype(BF16)
    low = (amp - high.astype(F32)).astype(BF16)
    total = jnp.dot(high, band_ref[...], preferred_element_type=F32) + jnp.dot(
        low, band_ref[...], preferred_element_type=F32
    )
    factor = 1.0 / (total * (1.0 / (2 * SMOOTH + 1)) + 1e-06)
    white[:, :MAIN] = re * factor[:, :MAIN]
    white[:, MAIN : 2 * MAIN] = im * factor[:, :MAIN]
    white[:, 2 * MAIN :] = tail * factor[:, MAIN:]

    place = lax.axis_index("tm")
    z, core = place // 2, lax.rem(place, 2)
    row_id = lax.broadcasted_iota(jnp.int32, (SRC_ROWS, WIDTH), 0)
    source = jnp.zeros((SRC_ROWS, WIDTH), F32)
    for s in range(src_ref.shape[1]):
        source = jnp.where(row_id == s, white[pl.ds(src_ref[0, s], 1), :], source)

    def share(d, q, start, size):
        owner = jnp.bitwise_xor(z, d) * 2 + jnp.bitwise_xor(core, q)
        return white[pl.ds(pl.multiple_of(owner * shared + start, 8), size), :]

    first, second = chunks
    for d in range(zs):
        block = [share(d, 0, 0, first), share(d, 1, 0, first), source]
        outs[d][...] = jnp.concatenate(block, axis=0).astype(BF16)
        for q in range(2):
            outs[zs + 2 * d + q][...] = share(d, q, first, second).astype(BF16)


def pack_kernel(sources, first, *refs):
    ins, out = refs[:-1], refs[-1]
    parts = [ref[...].astype(F32)[2 * first : 2 * first + sources] for ref in ins]
    out[...] = jnp.concatenate(parts, axis=0).astype(BF16)


def cross_kernel(count, windows, sources, parts, *refs):
    src_refs = refs[:count]
    rec_refs = refs[count : count + windows]
    high_ref, low_ref = refs[count + windows : count + windows + 2]
    outs = refs[count + windows + 2 : 2 * count + windows + 2]
    rec, src, stack = refs[2 * count + windows + 2 :]
    size = parts[0][1]
    for w in range(windows):
        start = parts[w][0]
        rec[pl.ds(w * size, size), :WIDTH] = rec_refs[w][...].astype(F32)[start : start + size]
        part = rec[pl.ds(w * size, size), 2 * MAIN : WIDTH]
        rec[pl.ds(w * size, size), WIDTH:] = pltpu.roll(part, TAIL, 1)
    per = windows * sources
    for b in range(count):
        src[pl.ds(b * per, per), :] = src_refs[b][...].astype(F32)
    step = 16 if size % 16 == 0 else 8
    for b in range(count):
        for s in range(sources):
            for g in range(0, size, step):
                totals = [0.0] * 4
                for w in range(windows):
                    a = src[pl.ds(b * per + w * sources + s, 1), :]
                    r = rec[pl.ds(w * size + g, step), :]
                    a_re, a_im, a_tail = a[:, :MAIN], a[:, MAIN : 2 * MAIN], a[:, 2 * MAIN :]
                    r_re, r_im = r[:, :MAIN], r[:, MAIN : 2 * MAIN]
                    totals[0] += a_re * r_re + a_im * r_im
                    totals[1] += a_re * r_im - a_im * r_re
                    totals[2] += a_tail * r[:, 2 * MAIN : WIDTH]
                    totals[3] += a_tail * r[:, WIDTH:]
                stack[pl.ds((b * sources + s) * size + g, step), :] = jnp.concatenate(totals, axis=1)
    cross = stack[...]
    high = cross.astype(BF16)
    low = (cross - high.astype(F32)).astype(BF16)
    lag_high, lag_low = high_ref[...], low_ref[...]
    lagged = (
        jnp.dot(high, lag_high, preferred_element_type=F32)
        + jnp.dot(low, lag_high, preferred_element_type=F32)
        + jnp.dot(high, lag_low, preferred_element_type=F32)
    )
    for b in range(count):
        outs[b][...] = lagged[b * sources * size : (b + 1) * sources * size].astype(BF16)


def finish_kernel(count, chunks, sources, partner_ref, counts_ref, *refs):
    ins, out = refs[:-1], refs[-1]
    me = lax.axis_index("chan")
    slots = partner_ref.shape[1]
    start = 0
    for i, size in enumerate(chunks):
        for p in range(slots):
            wanted = jnp.bitwise_xor(partner_ref[0, p], me)
            wanted = jnp.where(p < counts_ref[0], wanted, -1)
            value = jnp.zeros((sources * size, 2 * HL), F32)
            for e in range(count):
                value = jnp.where(wanted == e, ins[i * count + e][...].astype(F32), value)
            for s in range(sources):
                out[pl.ds(start, size), p, s, :] = value[s * size : (s + 1) * size]
        start += size


def call(kernel, out_shape, scratch, args, smem=0):
    specs = [pl.BlockSpec(memory_space=pltpu.SMEM)] * smem
    specs += [pl.BlockSpec(memory_space=pltpu.VMEM)] * (len(args) - smem)
    return pl.pallas_call(
        kernel,
        out_shape=out_shape,
        in_specs=specs,
        out_specs=jax.tree.map(lambda _: pl.BlockSpec(memory_space=pltpu.VMEM), out_shape),
        scratch_shapes=scratch,
        compiler_params=pltpu.CompilerParams(vmem_limit_bytes=40 * 1024 * 1024),
    )(*args)


def swap(value, axis, size, distance):
    return lax.ppermute(value, axis, [(i, i ^ distance) for i in range(size)])


def local(chans, tms, records, partners, counts, sources):
    channels = records.shape[1]
    picked = sources.shape[1]
    shared = channels // tms
    zs = tms // 2
    first = max(8, shared // 3 // 8 * 8)
    chunks = (first, shared - first)
    second = chunks[1]
    shape = jax.ShapeDtypeStruct
    high, low = lag_tables(1.0 / math.sqrt(F * tms))

    sent = call(
        functools.partial(whiten_kernel, chunks, shared, zs),
        [shape((2 * first + SRC_ROWS, WIDTH), BF16)] * zs + [shape((second, WIDTH), BF16)] * tms,
        [pltpu.VMEM((channels, WIDTH), F32)],
        (sources, records[0], jnp.asarray(dft_table()), jnp.asarray(band_table())),
        smem=1,
    )
    sent_one, sent_two = sent[:zs], sent[zs:]
    one = [sent_one[0]] + [None] * (zs - 1)
    for d in sorted(range(1, zs), key=lambda d: d == 1):
        one[d] = swap(sent_one[d], "tm", tms, 2 * d)
    two = [sent_two[0]] + [swap(sent_two[d], "tm", tms, d) for d in range(1, tms)]
    other = [swap(value, "tm", tms, 1) for value in one]

    own = call(
        functools.partial(pack_kernel, picked, first),
        shape((tms * picked, WIDTH), BF16),
        [],
        one + other,
    )
    spectra = [own] + [swap(own, "chan", chans, e) for e in range(1, chans)]

    def cross(receivers, parts):
        size = parts[0][1]
        return call(
            functools.partial(cross_kernel, chans, tms, picked, parts),
            [shape((picked * size, 2 * HL), BF16)] * chans,
            [
                pltpu.VMEM((tms * size, WIDTH + LANES), F32),
                pltpu.VMEM((chans * tms * picked, WIDTH), F32),
                pltpu.VMEM((chans * picked * size, WIDTH + LANES), F32),
            ],
            (*spectra, *receivers, jnp.asarray(high), jnp.asarray(low)),
        )

    done_one = cross(one + other, [(0, first)] * zs + [(first, first)] * zs)
    order = list(range(0, tms, 2)) + list(range(1, tms, 2))
    done_two = cross([two[d] for d in order], [(0, second)] * tms)
    arrived = []
    for done in (done_one, done_two):
        arrived += [done[0]] + [swap(done[e], "chan", chans, e) for e in range(1, chans)]
    result = call(
        functools.partial(finish_kernel, chans, chunks, picked),
        shape((shared, partners.shape[1], picked, 2 * HL), F32),
        [],
        (partners, counts, *arrived),
        smem=2,
    )
    return result[None]


def solution(mesh):
    sizes = dict(mesh.shape)
    return jax.shard_map(
        functools.partial(local, sizes["chan"], sizes["tm"]),
        mesh=mesh,
        in_specs=(P("tm", "chan", None), P("chan", None), P("chan"), P("chan", None)),
        out_specs=P("chan", "tm", None, None, None),
        check_vma=False,
    )
```

```python
import functools
import math

import jax
import jax.numpy as jnp
import ml_dtypes
import numpy as np
from jax import lax
from jax.experimental import pallas as pl
from jax.experimental.pallas import tpu as pltpu
from jax.sharding import PartitionSpec as P

L = 1536
F = 320
HL = 192
SMOOTH = 32
LANES = 128
TAIL = F % LANES
MAIN = F - TAIL
WIDTH = 2 * F
HALF = L // 2
SRC_ROWS = 8
F32 = jnp.float32
BF16 = jnp.bfloat16


def dft_half():
    n = np.arange(HALF)[:, None]
    k = np.arange(F)[None, :] + 1
    angle = (n * k % L).astype(np.float32) * np.float32(2.0 * math.pi / L)
    c, s = np.cos(angle), -np.sin(angle)
    table = np.concatenate([c[:, :MAIN], s[:, :MAIN], c[:, MAIN:], s[:, MAIN:]], axis=1)
    return table.astype(ml_dtypes.bfloat16)


def band_table():
    bins = np.concatenate([np.arange(F), np.arange(MAIN, F)])
    centre = np.clip(bins, SMOOTH, F - 1 - SMOOTH)
    band = np.abs(bins[:, None] - centre[None, :]) <= SMOOTH
    band[F:] = False
    return band.astype(ml_dtypes.bfloat16)


def lag_tables(scale):
    k = np.arange(F)[:, None] + 1
    j = np.arange(2 * HL)[None, :] - HL
    angle = np.mod(k * j, L).astype(np.float32) * np.float32(2.0 * math.pi / L)
    c, s = np.cos(angle) * np.float32(scale), -np.sin(angle) * np.float32(scale)
    table = np.concatenate([c[:MAIN], s[:MAIN], c[MAIN:], c[MAIN:], s[MAIN:], -s[MAIN:]], axis=0)
    high = table.astype(ml_dtypes.bfloat16)
    low = (table - high.astype(np.float32)).astype(ml_dtypes.bfloat16)
    return np.concatenate([high, low], axis=0)


def whiten(signal, tab, band):
    rows = signal.shape[0]
    signal = (signal - jnp.sum(signal, axis=1, keepdims=True) * (1.0 / L)).astype(BF16)
    halves = jnp.concatenate([signal[:, :HALF], signal[:, HALF:]], axis=0)
    spec = jnp.dot(halves, tab[...], preferred_element_type=F32)
    lane = lax.broadcasted_iota(jnp.int32, (1, WIDTH), 1)
    spec = spec[:rows] + jnp.where(lane % 2 == 1, 1.0, -1.0).astype(F32) * spec[rows:]
    re, im, tail = spec[:, :MAIN], spec[:, MAIN : 2 * MAIN], spec[:, 2 * MAIN :]
    tail_sq = tail * tail
    amp = jnp.sqrt(
        jnp.concatenate([re * re + im * im, tail_sq + pltpu.roll(tail_sq, TAIL, 1)], axis=1)
    )
    high = amp.astype(BF16)
    low = (amp - high.astype(F32)).astype(BF16)
    total = jnp.dot(high, band[...], preferred_element_type=F32) + jnp.dot(
        low, band[...], preferred_element_type=F32
    )
    factor = 1.0 / (total * (1.0 / (2 * SMOOTH + 1)) + 1e-06)
    return re * factor[:, :MAIN], im * factor[:, :MAIN], tail * factor[:, MAIN:]


def keep(ref, here, parts):
    ref[here, :MAIN], ref[here, MAIN : 2 * MAIN], ref[here, 2 * MAIN :] = parts


def whiten_kernel(layout, shared, src_hbm, rec_hbm, tab_hbm, band_hbm, *rest):
    outs = rest[: len(layout)]
    rec, tab, band, white, picked, sem = rest[len(layout) :]
    loads = [
        pltpu.make_async_copy(*pair, sem.at[i])
        for i, pair in enumerate(
            [(rec_hbm.at[0], rec), (tab_hbm, tab), (src_hbm, picked), (band_hbm, band)]
        )
    ]
    for load in loads:
        load.start()
    loads[0].wait()
    signal = rec[...].astype(F32)
    for load in loads[1:]:
        load.wait()
    keep(white, slice(None), whiten(signal, tab, band))
    place = lax.axis_index("tm")
    chip, core = place // 2, lax.rem(place, 2)
    row_id = lax.broadcasted_iota(jnp.int32, (SRC_ROWS, WIDTH), 0)
    source = jnp.zeros((SRC_ROWS, WIDTH), F32)
    for s in range(picked.shape[1]):
        source = jnp.where(row_id == s, white[pl.ds(picked[0, s], 1), :], source)
    for out, (d, first, size, with_source) in zip(outs, layout):
        rows = []
        for q in range(2):
            owner = jnp.bitwise_xor(chip, d) * 2 + jnp.bitwise_xor(core, q)
            if size:
                rows.append(white[pl.ds(pl.multiple_of(owner * shared + first, 8), size), :])
        if with_source:
            rows.append(source)
        out[...] = jnp.concatenate(rows, axis=0).astype(BF16)


def gather_kernel(size, *refs):
    ins, out = refs[:-1], refs[-1]
    parts = [ref[...].astype(F32)[2 * size :] for ref in ins]
    out[...] = jnp.concatenate(parts, axis=0).astype(BF16)


def hold_kernel(first, rest, count, *refs):
    out = refs[-1]
    parts = [ref[...].astype(F32)[first : 2 * first] for ref in refs[:count] if first]
    parts += [ref[...].astype(F32)[rest:] for ref in refs[count : 2 * count]]
    out[...] = jnp.concatenate(parts, axis=0).astype(BF16)


def pack_kernel(start, sources, here, there, out):
    parts = []
    for ref in (here, there):
        value = ref[...].astype(F32)[start:]
        parts += [value[i : i + sources] for i in range(0, value.shape[0], SRC_ROWS)]
    out[...] = jnp.concatenate(parts, axis=0).astype(BF16)


def cross_kernel(count, windows, sources, size, parts, *refs):
    src_refs = refs[:count]
    rec_refs = refs[count : count + len(parts)]
    lag_hbm = refs[count + len(parts)]
    outs = refs[count + len(parts) + 1 : 2 * count + len(parts) + 1]
    rec, src, stack, lag, sem = refs[2 * count + len(parts) + 1 :]
    lag_load = pltpu.make_async_copy(lag_hbm, lag, sem)
    lag_load.start()
    for ref, places in zip(rec_refs, parts):
        rows = ref[...].astype(F32)
        for w, start, place, length in places:
            value = rows[start : start + length]
            here = pl.ds(w * size + place, length)
            rec[here, :WIDTH] = value
            rec[here, WIDTH:] = pltpu.roll(value[:, 2 * MAIN :], TAIL, 1)
    per = windows * sources
    for b in range(count):
        src[pl.ds(b * per, per), :] = src_refs[b][...].astype(F32)
    step = 16 if size % 16 == 0 else 8
    for b in range(count):
        for s in range(sources):
            for g in range(0, size, step):
                totals = [0.0] * 4
                for w in range(windows):
                    a = src[pl.ds(b * per + w * sources + s, 1), :]
                    r = rec[pl.ds(w * size + g, step), :]
                    a_re, a_im, a_tail = a[:, :MAIN], a[:, MAIN : 2 * MAIN], a[:, 2 * MAIN :]
                    r_re, r_im = r[:, :MAIN], r[:, MAIN : 2 * MAIN]
                    totals[0] += a_re * r_re + a_im * r_im
                    totals[1] += a_re * r_im - a_im * r_re
                    totals[2] += a_tail * r[:, 2 * MAIN : WIDTH]
                    totals[3] += a_tail * r[:, WIDTH:]
                stack[pl.ds((b * sources + s) * size + g, step), :] = jnp.concatenate(totals, axis=1)
    cross = stack[...]
    high = cross.astype(BF16)
    low = (cross - high.astype(F32)).astype(BF16)
    lag_load.wait()
    lag_high, lag_low = lag[: WIDTH + LANES], lag[WIDTH + LANES :]
    lagged = (
        jnp.dot(high, lag_high, preferred_element_type=F32)
        + jnp.dot(low, lag_high, preferred_element_type=F32)
        + jnp.dot(high, lag_low, preferred_element_type=F32)
    )
    for b in range(count):
        outs[b][...] = lagged[b * sources * size : (b + 1) * sources * size].astype(BF16)


def finish_kernel(count, sources, partner_ref, counts_ref, *refs):
    ins, out = refs[:-1], refs[-1]
    me = lax.axis_index("chan")
    slots = partner_ref.shape[1]
    size = out.shape[0]
    for p in range(slots):
        wanted = jnp.bitwise_xor(partner_ref[0, p], me)
        wanted = jnp.where(p < counts_ref[0], wanted, -1)
        value = jnp.zeros((sources * size, 2 * HL), F32)
        for e in range(count):
            value = jnp.where(wanted == e, ins[e][...].astype(F32), value)
        for s in range(sources):
            out[:, p, s, :] = value[s * size : (s + 1) * size]


def in_hbm(value):
    return pltpu.with_memory_space_constraint(value, pltpu.HBM)


def call(kernel, out_shape, scratch, spaces, args):
    return pl.pallas_call(
        kernel,
        out_shape=out_shape,
        in_specs=[pl.BlockSpec(memory_space=space) for space in spaces],
        out_specs=jax.tree.map(lambda _: pl.BlockSpec(memory_space=pltpu.VMEM), out_shape),
        scratch_shapes=scratch,
        compiler_params=pltpu.CompilerParams(vmem_limit_bytes=40 * 1024 * 1024),
    )(*args)


def swap(value, axis, size, distance):
    return lax.ppermute(value, axis, [(i, i ^ distance) for i in range(size)])


def local(chans, tms, records, partners, counts, sources):
    channels = records.shape[1]
    picked = sources.shape[1]
    shared = channels // tms
    zs = tms // 2
    size = 2 * shared
    shape = jax.ShapeDtypeStruct
    vmem, smem, hbm = pltpu.VMEM, pltpu.SMEM, pltpu.HBM

    table, band = dft_half(), band_table()
    first = 16
    rest = shared - first
    layout = [(d, 0, first, True) for d in range(zs)]
    layout += [(d, first, rest, False) for d in range(zs)]
    rows = [2 * n + (SRC_ROWS if src else 0) for _, _, n, src in layout]
    sent = call(
        functools.partial(whiten_kernel, layout, shared),
        [shape((n, WIDTH), BF16) for n in rows],
        [
            pltpu.VMEM((channels, L), BF16),
            pltpu.VMEM(table.shape, BF16),
            pltpu.VMEM(band.shape, BF16),
            pltpu.VMEM((channels, WIDTH), F32),
            pltpu.SMEM(sources.shape, jnp.int32),
            pltpu.SemaphoreType.DMA((4,)),
        ],
        [hbm] * 4,
        tuple(in_hbm(v) for v in (sources, records, jnp.asarray(table), jnp.asarray(band))),
    )

    def across(values):
        return [v if d == 0 else swap(v, "tm", tms, 2 * d) for d, v in enumerate(values)]

    one, two = across(sent[:zs]), across(sent[zs:])
    gathered = call(
        functools.partial(gather_kernel, first),
        shape((zs * SRC_ROWS, WIDTH), BF16),
        [],
        [vmem] * zs,
        one,
    )
    other_one = swap(gathered, "tm", tms, 1)
    own = call(
        functools.partial(pack_kernel, 0, picked),
        shape((tms * picked, WIDTH), BF16),
        [],
        [vmem] * 2,
        [gathered, other_one],
    )
    spectra = [own] + [swap(own, "chan", chans, e) for e in range(1, chans)]
    deps = spectra[1:]
    gathered = call(
        functools.partial(hold_kernel, first, rest, zs),
        shape((zs * shared, WIDTH), BF16),
        [],
        [vmem] * (2 * zs + len(deps)),
        one + two + deps,
    )
    other_two = swap(gathered, "tm", tms, 1)
    receivers, parts = [], []
    for values, start, size in ((one, 0, first), (two, first, rest)):
        if size:
            receivers += values
            parts += [[(d, 0, start, size)] for d in range(zs)]
    receivers.append(other_two)
    places = [(zs + d, d * first, 0, first) for d in range(zs) if first]
    places += [(zs + d, zs * first + d * rest, first, rest) for d in range(zs)]
    parts.append(places)

    lags = lag_tables(1.0 / math.sqrt(F * tms))
    done = call(
        functools.partial(cross_kernel, chans, tms, picked, shared, parts),
        [shape((picked * shared, 2 * HL), BF16)] * chans,
        [
            pltpu.VMEM((tms * shared, WIDTH + LANES), F32),
            pltpu.VMEM((chans * tms * picked, WIDTH), F32),
            pltpu.VMEM((chans * picked * shared, WIDTH + LANES), F32),
            pltpu.VMEM(lags.shape, BF16),
            pltpu.SemaphoreType.DMA,
        ],
        [vmem] * (chans + len(receivers)) + [hbm],
        (*spectra, *receivers, in_hbm(jnp.asarray(lags))),
    )
    arrived = [done[0]] + [swap(done[e], "chan", chans, e) for e in range(1, chans)]
    result = call(
        functools.partial(finish_kernel, chans, picked),
        shape((shared, partners.shape[1], picked, 2 * HL), F32),
        [],
        [smem] * 2 + [vmem] * chans,
        (partners, counts, *arrived),
    )
    return result[None]


def solution(mesh):
    sizes = dict(mesh.shape)
    return jax.shard_map(
        functools.partial(local, sizes["chan"], sizes["tm"]),
        mesh=mesh,
        in_specs=(P("tm", "chan", None), P("chan", None), P("chan"), P("chan", None)),
        out_specs=P("chan", "tm", None, None, None),
        check_vma=False,
    )
```

```python
import functools
import math

import jax
import jax.numpy as jnp
import ml_dtypes
import numpy as np
from jax import lax
from jax.experimental import pallas as pl
from jax.experimental.pallas import tpu as pltpu
from jax.sharding import PartitionSpec as P

L = 1536
F = 320
HL = 192
SMOOTH = 32
LANES = 128
TAIL = F % LANES
MAIN = F - TAIL
WIDTH = 2 * F
HALF = L // 2
SRC_ROWS = 8
F32 = jnp.float32
BF16 = jnp.bfloat16


def dft_half():
    n = np.arange(HALF)[:, None]
    k = np.arange(F)[None, :] + 1
    angle = (n * k % L).astype(np.float32) * np.float32(2.0 * math.pi / L)
    c, s = np.cos(angle), -np.sin(angle)
    table = np.concatenate([c[:, :MAIN], s[:, :MAIN], c[:, MAIN:], s[:, MAIN:]], axis=1)
    return table.astype(ml_dtypes.bfloat16)


def band_table():
    bins = np.concatenate([np.arange(F), np.arange(MAIN, F)])
    centre = np.clip(bins, SMOOTH, F - 1 - SMOOTH)
    band = np.abs(bins[:, None] - centre[None, :]) <= SMOOTH
    band[F:] = False
    return band.astype(ml_dtypes.bfloat16)


def lag_tables(scale):
    k = np.arange(F)[:, None] + 1
    j = np.arange(2 * HL)[None, :] - HL
    angle = np.mod(k * j, L).astype(np.float32) * np.float32(2.0 * math.pi / L)
    c, s = np.cos(angle) * np.float32(scale), -np.sin(angle) * np.float32(scale)
    table = np.concatenate([c[:MAIN], s[:MAIN], c[MAIN:], c[MAIN:], s[MAIN:], -s[MAIN:]], axis=0)
    high = table.astype(ml_dtypes.bfloat16)
    low = (table - high.astype(np.float32)).astype(ml_dtypes.bfloat16)
    return np.concatenate([high, low], axis=0)


def whiten(signal, tab, band):
    rows = signal.shape[0]
    signal = (signal - jnp.sum(signal, axis=1, keepdims=True) * (1.0 / L)).astype(BF16)
    halves = jnp.concatenate([signal[:, :HALF], signal[:, HALF:]], axis=0)
    spec = jnp.dot(halves, tab[...], preferred_element_type=F32)
    lane = lax.broadcasted_iota(jnp.int32, (1, WIDTH), 1)
    spec = spec[:rows] + jnp.where(lane % 2 == 1, 1.0, -1.0).astype(F32) * spec[rows:]
    re, im, tail = spec[:, :MAIN], spec[:, MAIN : 2 * MAIN], spec[:, 2 * MAIN :]
    tail_sq = tail * tail
    amp = jnp.sqrt(
        jnp.concatenate([re * re + im * im, tail_sq + pltpu.roll(tail_sq, TAIL, 1)], axis=1)
    )
    high = amp.astype(BF16)
    low = (amp - high.astype(F32)).astype(BF16)
    total = jnp.dot(high, band[...], preferred_element_type=F32) + jnp.dot(
        low, band[...], preferred_element_type=F32
    )
    factor = 1.0 / (total * (1.0 / (2 * SMOOTH + 1)) + 1e-06)
    return re * factor[:, :MAIN], im * factor[:, :MAIN], tail * factor[:, MAIN:]


def keep(ref, here, parts):
    ref[here, :MAIN], ref[here, MAIN : 2 * MAIN], ref[here, 2 * MAIN :] = parts


def whiten_kernel(layout, shared, src_hbm, rec_hbm, tab_hbm, band_hbm, lag_hbm, *rest):
    outs = rest[: len(layout)]
    lag, rec, tab, band, white, picked, sem = rest[len(layout) :]
    loads = [
        pltpu.make_async_copy(*pair, sem.at[i])
        for i, pair in enumerate(
            [
                (rec_hbm.at[0], rec),
                (tab_hbm, tab),
                (src_hbm, picked),
                (band_hbm, band),
                (lag_hbm, lag),
            ]
        )
    ]
    for load in loads:
        load.start()
    loads[0].wait()
    signal = rec[...].astype(F32)
    for load in loads[1:-1]:
        load.wait()
    keep(white, slice(None), whiten(signal, tab, band))
    place = lax.axis_index("tm")
    chip, core = place // 2, lax.rem(place, 2)
    row_id = lax.broadcasted_iota(jnp.int32, (SRC_ROWS, WIDTH), 0)
    source = jnp.zeros((SRC_ROWS, WIDTH), F32)
    for s in range(picked.shape[1]):
        source = jnp.where(row_id == s, white[pl.ds(picked[0, s], 1), :], source)
    for out, (d, first, size, with_source) in zip(outs, layout):
        rows = []
        for q in range(2):
            owner = jnp.bitwise_xor(chip, d) * 2 + jnp.bitwise_xor(core, q)
            if size:
                rows.append(white[pl.ds(pl.multiple_of(owner * shared + first, 8), size), :])
        if with_source:
            rows.append(source)
        out[...] = jnp.concatenate(rows, axis=0).astype(BF16)
    loads[-1].wait()


def gather_kernel(size, *refs):
    ins, out = refs[:-1], refs[-1]
    parts = [ref[...].astype(F32)[2 * size :] for ref in ins]
    out[...] = jnp.concatenate(parts, axis=0).astype(BF16)


def hold_kernel(first, rest, count, *refs):
    out = refs[-1]
    parts = [ref[...].astype(F32)[first : 2 * first] for ref in refs[:count] if first]
    parts += [ref[...].astype(F32)[rest:] for ref in refs[count : 2 * count]]
    out[...] = jnp.concatenate(parts, axis=0).astype(BF16)


def pack_kernel(start, sources, here, there, out):
    parts = []
    for ref in (here, there):
        value = ref[...].astype(F32)[start:]
        parts += [value[i : i + sources] for i in range(0, value.shape[0], SRC_ROWS)]
    out[...] = jnp.concatenate(parts, axis=0).astype(BF16)


def cross_sums(count, windows, sources, size, src, rec, put):
    step = 16 if size % 16 == 0 else 8
    for b in range(count):
        for s in range(sources):
            for g in range(0, size, step):
                totals = [0.0] * 4
                for i, w in enumerate(windows):
                    a = src[pl.ds((b * tms_of(src, count, sources) + w) * sources + s, 1), :]
                    r = rec[pl.ds(i * size + g, step), :]
                    a_re, a_im, a_tail = a[:, :MAIN], a[:, MAIN : 2 * MAIN], a[:, 2 * MAIN :]
                    r_re, r_im = r[:, :MAIN], r[:, MAIN : 2 * MAIN]
                    totals[0] += a_re * r_re + a_im * r_im
                    totals[1] += a_re * r_im - a_im * r_re
                    totals[2] += a_tail * r[:, 2 * MAIN : WIDTH]
                    totals[3] += a_tail * r[:, WIDTH:]
                put(pl.ds((b * sources + s) * size + g, step), jnp.concatenate(totals, axis=1))


def tms_of(src, count, sources):
    return src.shape[0] // (count * sources)


def unpack_receivers(rec, rec_refs, parts, size):
    for ref, places in zip(rec_refs, parts):
        rows = ref[...].astype(F32)
        for w, start, place, length in places:
            value = rows[start : start + length]
            here = pl.ds(w * size + place, length)
            rec[here, :WIDTH] = value
            rec[here, WIDTH:] = pltpu.roll(value[:, 2 * MAIN :], TAIL, 1)


def here_kernel(count, windows, sources, size, parts, arrays, *refs):
    src_refs, rec_refs = refs[:arrays], refs[arrays : arrays + len(parts)]
    stack, src, rec = refs[arrays + len(parts) :]
    start = 0
    for ref in src_refs:
        src[pl.ds(start, ref.shape[0]), :] = ref[...].astype(F32)
        start += ref.shape[0]
    unpack_receivers(rec, rec_refs, parts, size)

    def put(here, value):
        stack[here, :] = value

    cross_sums(count, windows, sources, size, src, rec, put)


def there_kernel(count, windows, sources, size, parts, half, src, *refs):
    rec_refs = refs[: len(parts)]
    lag = refs[len(parts)]
    outs = refs[len(parts) + 1 : len(parts) + 1 + count]
    rec, stack = refs[len(parts) + 1 + count :]
    unpack_receivers(rec, rec_refs, parts, size)

    def put(here, value):
        stack[here, :] = half[here, :] + value

    cross_sums(count, windows, sources, size, src, rec, put)
    cross = stack[...]
    high = cross.astype(BF16)
    low = (cross - high.astype(F32)).astype(BF16)
    lag_high, lag_low = lag[: WIDTH + LANES], lag[WIDTH + LANES :]
    lagged = (
        jnp.dot(high, lag_high, preferred_element_type=F32)
        + jnp.dot(low, lag_high, preferred_element_type=F32)
        + jnp.dot(high, lag_low, preferred_element_type=F32)
    )
    for b in range(count):
        outs[b][...] = lagged[b * sources * size : (b + 1) * sources * size].astype(BF16)


def wanted_kernel(partner, live, _, wanted):
    me = lax.axis_index("chan")
    row_id = lax.broadcasted_iota(jnp.int32, wanted.shape, 0)
    distance = jnp.full(wanted.shape, -1, jnp.int32)
    for p in range(partner.shape[1]):
        value = jnp.where(p < live[0], jnp.bitwise_xor(partner[0, p], me), -1)
        distance = jnp.where(row_id == p, value, distance)
    wanted[...] = distance


def finish_kernel(order, slots, sources, wanted_ref, *refs):
    ins, out = refs[:-1], refs[-1]
    size = out.shape[0]
    for p in range(slots):
        wanted = jnp.broadcast_to(wanted_ref[p : p + 1, :1], (1, 2 * HL))
        value = jnp.zeros((sources * size, 2 * HL), F32)
        for e, ref in zip(order, ins):
            value = jnp.where(wanted == e, ref[...].astype(F32), value)
        for s in range(sources):
            out[:, p, s, :] = value[s * size : (s + 1) * size]


def in_hbm(value):
    return pltpu.with_memory_space_constraint(value, pltpu.HBM)


def call(kernel, out_shape, scratch, spaces, args):
    return pl.pallas_call(
        kernel,
        out_shape=out_shape,
        in_specs=[pl.BlockSpec(memory_space=space) for space in spaces],
        out_specs=jax.tree.map(lambda _: pl.BlockSpec(memory_space=pltpu.VMEM), out_shape),
        scratch_shapes=scratch,
        compiler_params=pltpu.CompilerParams(vmem_limit_bytes=40 * 1024 * 1024),
    )(*args)


def swap(value, axis, size, distance):
    return lax.ppermute(value, axis, [(i, i ^ distance) for i in range(size)])


def local(chans, tms, records, partners, counts, sources):
    channels = records.shape[1]
    picked = sources.shape[1]
    shared = channels // tms
    zs = tms // 2
    size = 2 * shared
    shape = jax.ShapeDtypeStruct
    vmem, smem, hbm = pltpu.VMEM, pltpu.SMEM, pltpu.HBM

    table, band = dft_half(), band_table()
    first = 16
    rest = shared - first
    order = sorted(range(zs), key=lambda d: (d == 1, d))
    layout = [(d, 0, first, True) for d in order]
    layout += [(d, first, rest, False) for d in order]
    rows = [2 * n + (SRC_ROWS if src else 0) for _, _, n, src in layout]
    lags = lag_tables(1.0 / math.sqrt(F * tms))
    *sent, lags = call(
        functools.partial(whiten_kernel, layout, shared),
        [shape((n, WIDTH), BF16) for n in rows] + [shape(lags.shape, BF16)],
        [
            pltpu.VMEM((channels, L), BF16),
            pltpu.VMEM(table.shape, BF16),
            pltpu.VMEM(band.shape, BF16),
            pltpu.VMEM((channels, WIDTH), F32),
            pltpu.SMEM(sources.shape, jnp.int32),
            pltpu.SemaphoreType.DMA((5,)),
        ],
        [hbm] * 5,
        (
            *(in_hbm(value) for value in (sources, records)),
            *(in_hbm(jnp.asarray(constant)) for constant in (table, band, lags)),
        ),
    )

    def across(values):
        return [v if d == 0 else swap(v, "tm", tms, 2 * d) for d, v in zip(order, values)]

    one, two = across(sent[:zs]), across(sent[zs:])
    gathered = call(
        functools.partial(gather_kernel, first),
        shape((zs * SRC_ROWS, WIDTH), BF16),
        [],
        [vmem] * zs,
        one,
    )
    other_one = swap(gathered, "tm", tms, 1)
    own = call(
        functools.partial(pack_kernel, 0, picked),
        shape((tms * picked, WIDTH), BF16),
        [],
        [vmem] * 2,
        [gathered, other_one],
    )
    blocks = list(reversed(range(chans)))
    spectra = [own if e == 0 else swap(own, "chan", chans, e) for e in blocks]
    deps = spectra[:-1]
    gathered = call(
        functools.partial(hold_kernel, first, rest, zs),
        shape((zs * shared, WIDTH), BF16),
        [],
        [vmem] * (2 * zs + len(deps)),
        one + two + deps,
    )
    other_two = swap(gathered, "tm", tms, 1)
    receivers, parts = [], []
    for values, start, size in ((one, 0, first), (two, first, rest)):
        if size:
            receivers += values
            parts += [[(d, 0, start, size)] for d in range(zs)]
    pairs = chans * picked * shared
    half, src = call(
        functools.partial(
            here_kernel, chans, range(zs), picked, shared, parts, len(spectra)
        ),
        [shape((pairs, WIDTH + LANES), F32), shape((chans * tms * picked, WIDTH), F32)],
        [pltpu.VMEM((zs * shared, WIDTH + LANES), F32)],
        [vmem] * (len(spectra) + len(receivers)),
        (*spectra, *receivers),
    )
    places = [(d, d * first, 0, first) for d in range(zs) if first]
    places += [(d, zs * first + d * rest, first, rest) for d in range(zs)]
    done = call(
        functools.partial(there_kernel, chans, range(zs, tms), picked, shared, [places]),
        [shape((picked * shared, 2 * HL), BF16)] * chans,
        [
            pltpu.VMEM((zs * shared, WIDTH + LANES), F32),
            pltpu.VMEM((pairs, WIDTH + LANES), F32),
        ],
        [vmem] * 4,
        (half, src, other_two, lags),
    )
    done = dict(zip(blocks, done))
    ways = list(range(2, chans)) + [1, 0] if chans > 1 else [0]
    arrived = [done[e] if e == 0 else swap(done[e], "chan", chans, e) for e in ways]
    slots = partners.shape[1]
    wanted = call(
        wanted_kernel,
        shape((-(-slots // 8) * 8, LANES), jnp.int32),
        [],
        [smem, smem, vmem],
        (partners, counts, done[0]),
    )
    result = call(
        functools.partial(finish_kernel, ways, slots, picked),
        shape((shared, slots, picked, 2 * HL), F32),
        [],
        [vmem] * (1 + chans),
        (wanted, *arrived),
    )
    return result[None]


def solution(mesh):
    sizes = dict(mesh.shape)
    return jax.shard_map(
        functools.partial(local, sizes["chan"], sizes["tm"]),
        mesh=mesh,
        in_specs=(P("tm", "chan", None), P("chan", None), P("chan"), P("chan", None)),
        out_specs=P("chan", "tm", None, None, None),
        check_vma=False,
    )
```

```python
import functools
import math

import jax
import jax.numpy as jnp
import ml_dtypes
import numpy as np
from jax import lax
from jax.experimental import pallas as pl
from jax.experimental.pallas import tpu as pltpu
from jax.sharding import PartitionSpec as P

L = 1536
F = 320
HL = 192
SMOOTH = 32
LANES = 128
TAIL = F % LANES
MAIN = F - TAIL
WIDTH = 2 * F
HALF = L // 2
SRC_ROWS = 8
F32 = jnp.float32
BF16 = jnp.bfloat16


def dft_half():
    n = np.arange(HALF)[:, None]
    k = np.arange(F)[None, :] + 1
    angle = (n * k % L).astype(np.float32) * np.float32(2.0 * math.pi / L)
    c, s = np.cos(angle), -np.sin(angle)
    table = np.concatenate([c[:, :MAIN], s[:, :MAIN], c[:, MAIN:], s[:, MAIN:]], axis=1)
    return table.astype(ml_dtypes.bfloat16)


def band_table():
    bins = np.concatenate([np.arange(F), np.arange(MAIN, F)])
    centre = np.clip(bins, SMOOTH, F - 1 - SMOOTH)
    band = np.abs(bins[:, None] - centre[None, :]) <= SMOOTH
    band[F:] = False
    return band.astype(ml_dtypes.bfloat16)


def lag_tables(scale):
    k = np.arange(F)[:, None] + 1
    j = np.arange(2 * HL)[None, :] - HL
    angle = np.mod(k * j, L).astype(np.float32) * np.float32(2.0 * math.pi / L)
    c, s = np.cos(angle) * np.float32(scale), -np.sin(angle) * np.float32(scale)
    table = np.concatenate([c[:MAIN], s[:MAIN], c[MAIN:], c[MAIN:], s[MAIN:], -s[MAIN:]], axis=0)
    high = table.astype(ml_dtypes.bfloat16)
    low = (table - high.astype(np.float32)).astype(ml_dtypes.bfloat16)
    return np.concatenate([high, low], axis=0)


def whiten(signal, tab, band):
    signal = (signal - jnp.sum(signal, axis=1, keepdims=True) * (1.0 / L)).astype(BF16)
    lane = lax.broadcasted_iota(jnp.int32, (1, WIDTH), 1)
    sign = jnp.where(lane % 2 == 1, 1.0, -1.0).astype(F32)
    spec = jnp.dot(signal[:, :HALF], tab[...], preferred_element_type=F32)
    spec = spec + sign * jnp.dot(signal[:, HALF:], tab[...], preferred_element_type=F32)
    re, im, tail = spec[:, :MAIN], spec[:, MAIN : 2 * MAIN], spec[:, 2 * MAIN :]
    tail_sq = tail * tail
    amp = jnp.sqrt(
        jnp.concatenate([re * re + im * im, tail_sq + pltpu.roll(tail_sq, TAIL, 1)], axis=1)
    )
    high = amp.astype(BF16)
    low = (amp - high.astype(F32)).astype(BF16)
    total = jnp.dot(high, band[...], preferred_element_type=F32) + jnp.dot(
        low, band[...], preferred_element_type=F32
    )
    factor = 1.0 / (total * (1.0 / (2 * SMOOTH + 1)) + 1e-06)
    return re * factor[:, :MAIN], im * factor[:, :MAIN], tail * factor[:, MAIN:]


def keep(ref, here, parts):
    ref[here, :MAIN], ref[here, MAIN : 2 * MAIN], ref[here, 2 * MAIN :] = parts


def whiten_kernel(layout, shared, src_hbm, rec_hbm, tab_hbm, band_hbm, lag_hbm, *rest):
    outs = rest[: len(layout)]
    lag, rec, tab, band, white, picked, sem = rest[len(layout) :]
    loads = [
        pltpu.make_async_copy(*pair, sem.at[i])
        for i, pair in enumerate(
            [
                (rec_hbm.at[0], rec),
                (tab_hbm, tab),
                (src_hbm, picked),
                (band_hbm, band),
                (lag_hbm, lag),
            ]
        )
    ]
    for load in loads:
        load.start()
    loads[0].wait()
    signal = rec[...].astype(F32)
    for load in loads[1:-1]:
        load.wait()
    keep(white, slice(None), whiten(signal, tab, band))
    place = lax.axis_index("tm")
    chip, core = place // 2, lax.rem(place, 2)
    row_id = lax.broadcasted_iota(jnp.int32, (SRC_ROWS, WIDTH), 0)
    source = jnp.zeros((SRC_ROWS, WIDTH), F32)
    for s in range(picked.shape[1]):
        source = jnp.where(row_id == s, white[pl.ds(picked[0, s], 1), :], source)
    for out, (d, first, size, with_source) in zip(outs, layout):
        rows = []
        for q in range(2):
            owner = jnp.bitwise_xor(chip, d) * 2 + jnp.bitwise_xor(core, q)
            rows.append(white[pl.ds(pl.multiple_of(owner * shared + first, 8), size), :])
        if with_source:
            rows.append(source)
        out[...] = jnp.concatenate(rows, axis=0).astype(BF16)
    loads[-1].wait()


def pack_kernel(starts, sources, *refs):
    ins, out = refs[:-1], refs[-1]
    parts = [ref[...].astype(F32)[start : start + sources] for ref, start in zip(ins, starts)]
    spare = out.shape[0] - len(ins) * sources
    if spare:
        parts.append(jnp.zeros((spare, WIDTH), F32))
    out[...] = jnp.concatenate(parts, axis=0).astype(BF16)


def gather_kernel(sizes, *refs):
    ins, out = refs[:-1], refs[-1]
    count = len(sizes)
    parts = [ref[...].astype(F32)[n : 2 * n] for ref, n in zip(ins, sizes)]
    parts += [ref[...].astype(F32) for ref in ins[count:]]
    out[...] = jnp.concatenate(parts, axis=0).astype(BF16)


def cross_sums(count, windows, sources, size, src, rec, put):
    block = src.shape[0] // count
    step = 16 if size % 16 == 0 else 8
    for b in range(count):
        for s in range(sources):
            for g in range(0, size, step):
                totals = [0.0] * 4
                for w in range(windows):
                    a = src[pl.ds(b * block + w * sources + s, 1), :]
                    r = rec[pl.ds(w * size + g, step), :]
                    a_re, a_im, a_tail = a[:, :MAIN], a[:, MAIN : 2 * MAIN], a[:, 2 * MAIN :]
                    r_re, r_im = r[:, :MAIN], r[:, MAIN : 2 * MAIN]
                    totals[0] += a_re * r_re + a_im * r_im
                    totals[1] += a_re * r_im - a_im * r_re
                    totals[2] += a_tail * r[:, 2 * MAIN : WIDTH]
                    totals[3] += a_tail * r[:, WIDTH:]
                put(pl.ds((b * sources + s) * size + g, step), jnp.concatenate(totals, axis=1))


def put_receivers(rec, here, value):
    rec[here, :WIDTH] = value
    rec[here, WIDTH:] = pltpu.roll(value[:, 2 * MAIN :], TAIL, 1)


def here_kernel(count, windows, sources, size, places, *refs):
    rec_refs, src_refs = refs[: len(places)], refs[len(places) : len(places) + count]
    stack, rec, src = refs[len(places) + count :]
    for ref, (start, n) in zip(rec_refs, places):
        put_receivers(rec, pl.ds(start, n), ref[...].astype(F32)[:n])
    block = src.shape[0] // count
    for b, ref in enumerate(src_refs):
        src[pl.ds(b * block, block), :] = ref[...].astype(F32)

    def put(here, value):
        stack[here, :] = value

    cross_sums(count, windows, sources, size, src, rec, put)


def there_kernel(count, windows, sources, size, places, half, other, lag, *refs):
    outs, (rec, src, stack) = refs[:count], refs[count:]
    rows = other[...].astype(F32)
    first = 0
    for start, n in places:
        put_receivers(rec, pl.ds(start, n), rows[first : first + n])
        first += n
    src[...] = rows[first:]

    pairs = half.shape[0]

    def put(here, value):
        value = half[here, :] + value
        high = value.astype(BF16)
        stack[here, :] = high
        stack[pl.ds(pairs + here.start, here.size), :] = (value - high.astype(F32)).astype(BF16)

    cross_sums(count, windows, sources, size, src, rec, put)
    lag_high, lag_low = lag[: WIDTH + LANES], lag[WIDTH + LANES :]
    both = jnp.dot(stack[...], lag_high, preferred_element_type=F32)
    lagged = both[:pairs] + both[pairs:]
    lagged = lagged + jnp.dot(stack[:pairs, :], lag_low, preferred_element_type=F32)
    for b in range(count):
        outs[b][...] = lagged[b * sources * size : (b + 1) * sources * size].astype(BF16)


def wanted_kernel(partner, live, _, wanted):
    me = lax.axis_index("chan")
    row_id = lax.broadcasted_iota(jnp.int32, wanted.shape, 0)
    distance = jnp.full(wanted.shape, -1, jnp.int32)
    for p in range(partner.shape[1]):
        value = jnp.where(p < live[0], jnp.bitwise_xor(partner[0, p], me), -1)
        distance = jnp.where(row_id == p, value, distance)
    wanted[...] = distance


def finish_kernel(order, slots, sources, wanted_ref, *refs):
    ins, out = refs[:-1], refs[-1]
    size = out.shape[0]
    for p in range(slots):
        wanted = jnp.broadcast_to(wanted_ref[p : p + 1, :1], (1, 2 * HL))
        value = jnp.zeros((sources * size, 2 * HL), F32)
        for e, ref in zip(order, ins):
            value = jnp.where(wanted == e, ref[...].astype(F32), value)
        for s in range(sources):
            out[:, p, s, :] = value[s * size : (s + 1) * size]


def in_hbm(value):
    return pltpu.with_memory_space_constraint(value, pltpu.HBM)


def call(kernel, out_shape, scratch, spaces, args):
    return pl.pallas_call(
        kernel,
        out_shape=out_shape,
        in_specs=[pl.BlockSpec(memory_space=space) for space in spaces],
        out_specs=jax.tree.map(lambda _: pl.BlockSpec(memory_space=pltpu.VMEM), out_shape),
        scratch_shapes=scratch,
        compiler_params=pltpu.CompilerParams(vmem_limit_bytes=40 * 1024 * 1024),
    )(*args)


def swap(value, axis, size, distance):
    return lax.ppermute(value, axis, [(i, i ^ distance) for i in range(size)])


def local(chans, tms, records, partners, counts, sources):
    channels = records.shape[1]
    picked = sources.shape[1]
    shared = channels // tms
    zs = tms // 2
    size = 2 * shared
    shape = jax.ShapeDtypeStruct
    vmem, smem, hbm = pltpu.VMEM, pltpu.SMEM, pltpu.HBM

    table, band = dft_half(), band_table()
    order = list(reversed(range(zs)))
    first = {d: max(8, shared // 16 * 8) for d in order}
    layout = [(d, 0, first[d], True) for d in order]
    late = [*range(1, zs), 0]
    layout += [(d, first[d], shared - first[d], False) for d in late]
    rows = [2 * n + (SRC_ROWS if src else 0) for _, _, n, src in layout]
    places = [(order.index(d) * shared + row, n) for d, row, n, _ in layout]
    lags = lag_tables(1.0 / math.sqrt(F * tms))
    *sent, lags = call(
        functools.partial(whiten_kernel, layout, shared),
        [shape((n, WIDTH), BF16) for n in rows] + [shape(lags.shape, BF16)],
        [
            pltpu.VMEM((channels, L), BF16),
            pltpu.VMEM(table.shape, BF16),
            pltpu.VMEM(band.shape, BF16),
            pltpu.VMEM((channels, WIDTH), F32),
            pltpu.SMEM(sources.shape, jnp.int32),
            pltpu.SemaphoreType.DMA((5,)),
        ],
        [hbm] * 5,
        (
            *(in_hbm(value) for value in (sources, records)),
            *(in_hbm(jnp.asarray(constant)) for constant in (table, band, lags)),
        ),
    )

    moved = [v if d == 0 else swap(v, "tm", tms, 2 * d) for (d, *_), v in zip(layout, sent)]
    block = -(-zs * picked // SRC_ROWS) * SRC_ROWS
    own = call(
        functools.partial(pack_kernel, [2 * first[d] for d in order], picked),
        shape((block, WIDTH), BF16),
        [],
        [vmem] * zs,
        moved[:zs],
    )
    blocks = list(range(2, chans)) + [1, 0]
    spectra = [own if e == 0 else swap(own, "chan", chans, e) for e in blocks]
    gathered = call(
        functools.partial(gather_kernel, [n for _, _, n, _ in layout]),
        shape((zs * shared + chans * block, WIDTH), BF16),
        [],
        [vmem] * (len(moved) + chans),
        moved + spectra,
    )
    other = swap(gathered, "tm", tms, 1)
    pairs = chans * picked * shared
    scratch = [
        pltpu.VMEM((zs * shared, WIDTH + LANES), F32),
        pltpu.VMEM((chans * block, WIDTH), F32),
    ]
    half = call(
        functools.partial(here_kernel, chans, zs, picked, shared, places),
        shape((pairs, WIDTH + LANES), F32),
        scratch,
        [vmem] * (len(moved) + chans),
        moved + spectra,
    )
    done = call(
        functools.partial(there_kernel, chans, zs, picked, shared, places),
        [shape((picked * shared, 2 * HL), BF16)] * chans,
        scratch + [pltpu.VMEM((2 * pairs, WIDTH + LANES), BF16)],
        [vmem] * 3,
        (half, other, lags),
    )
    done = dict(zip(blocks, done))
    ways = list(reversed(range(chans)))
    arrived = [done[e] if e == 0 else swap(done[e], "chan", chans, e) for e in ways]
    slots = partners.shape[1]
    wanted = call(
        wanted_kernel,
        shape((-(-slots // 8) * 8, LANES), jnp.int32),
        [],
        [smem, smem, vmem],
        (partners, counts, done[0]),
    )
    result = call(
        functools.partial(finish_kernel, ways, slots, picked),
        shape((shared, slots, picked, 2 * HL), F32),
        [],
        [vmem] * (1 + chans),
        (wanted, *arrived),
    )
    return result[None]


def solution(mesh):
    sizes = dict(mesh.shape)
    return jax.shard_map(
        functools.partial(local, sizes["chan"], sizes["tm"]),
        mesh=mesh,
        in_specs=(P("tm", "chan", None), P("chan", None), P("chan"), P("chan", None)),
        out_specs=P("chan", "tm", None, None, None),
        check_vma=False,
    )
```

```python
import functools
import math

import jax
import jax.numpy as jnp
import ml_dtypes
import numpy as np
from jax import lax
from jax.experimental import pallas as pl
from jax.experimental.pallas import tpu as pltpu
from jax.sharding import PartitionSpec as P

L = 1536
F = 320
HL = 192
SMOOTH = 32
LANES = 128
TAIL = F % LANES
MAIN = F - TAIL
WIDTH = 2 * F
HALF = L // 2
SRC_ROWS = 8
F32 = jnp.float32
BF16 = jnp.bfloat16


def dft_half():
    n = np.arange(HALF)[:, None]
    k = np.arange(F)[None, :] + 1
    angle = (n * k % L).astype(np.float32) * np.float32(2.0 * math.pi / L)
    c, s = np.cos(angle), -np.sin(angle)
    table = np.concatenate([c[:, :MAIN], s[:, :MAIN], c[:, MAIN:], s[:, MAIN:]], axis=1)
    return table.astype(ml_dtypes.bfloat16)


def band_table():
    bins = np.concatenate([np.arange(F), np.arange(MAIN, F)])
    centre = np.clip(bins, SMOOTH, F - 1 - SMOOTH)
    band = np.abs(bins[:, None] - centre[None, :]) <= SMOOTH
    band[F:] = False
    return band.astype(ml_dtypes.bfloat16)


def lag_tables(scale):
    k = np.arange(F)[:, None] + 1
    j = np.arange(2 * HL)[None, :] - HL
    angle = np.mod(k * j, L).astype(np.float32) * np.float32(2.0 * math.pi / L)
    c, s = np.cos(angle) * np.float32(scale), -np.sin(angle) * np.float32(scale)
    table = np.concatenate([c[:MAIN], s[:MAIN], c[MAIN:], c[MAIN:], s[MAIN:], -s[MAIN:]], axis=0)
    high = table.astype(ml_dtypes.bfloat16)
    low = (table - high.astype(np.float32)).astype(ml_dtypes.bfloat16)
    return np.concatenate([high, low], axis=0)


def whiten(signal, tab, band):
    signal = (signal - jnp.sum(signal, axis=1, keepdims=True) * (1.0 / L)).astype(BF16)
    lane = lax.broadcasted_iota(jnp.int32, (1, WIDTH), 1)
    sign = jnp.where(lane % 2 == 1, 1.0, -1.0).astype(F32)
    spec = jnp.dot(signal[:, :HALF], tab[...], preferred_element_type=F32)
    spec = spec + sign * jnp.dot(signal[:, HALF:], tab[...], preferred_element_type=F32)
    re, im, tail = spec[:, :MAIN], spec[:, MAIN : 2 * MAIN], spec[:, 2 * MAIN :]
    tail_sq = tail * tail
    amp = jnp.sqrt(
        jnp.concatenate([re * re + im * im, tail_sq + pltpu.roll(tail_sq, TAIL, 1)], axis=1)
    )
    high = amp.astype(BF16)
    low = (amp - high.astype(F32)).astype(BF16)
    total = jnp.dot(high, band[...], preferred_element_type=F32) + jnp.dot(
        low, band[...], preferred_element_type=F32
    )
    factor = 1.0 / (total * (1.0 / (2 * SMOOTH + 1)) + 1e-06)
    return re * factor[:, :MAIN], im * factor[:, :MAIN], tail * factor[:, MAIN:]


def keep(ref, here, parts):
    ref[here, :MAIN], ref[here, MAIN : 2 * MAIN], ref[here, 2 * MAIN :] = parts


def whiten_kernel(layout, shared, src_hbm, rec_hbm, tab_hbm, band_hbm, lag_hbm, *rest):
    outs = rest[: len(layout)]
    lag, rec, tab, band, white, picked, sem = rest[len(layout) :]
    loads = [
        pltpu.make_async_copy(*pair, sem.at[i])
        for i, pair in enumerate(
            [
                (rec_hbm.at[0], rec),
                (tab_hbm, tab),
                (src_hbm, picked),
                (band_hbm, band),
                (lag_hbm, lag),
            ]
        )
    ]
    for load in loads:
        load.start()
    loads[0].wait()
    signal = rec[...].astype(F32)
    for load in loads[1:-1]:
        load.wait()
    keep(white, slice(None), whiten(signal, tab, band))
    place = lax.axis_index("tm")
    chip, core = place // 2, lax.rem(place, 2)
    row_id = lax.broadcasted_iota(jnp.int32, (SRC_ROWS, WIDTH), 0)
    source = jnp.zeros((SRC_ROWS, WIDTH), F32)
    for s in range(picked.shape[1]):
        source = jnp.where(row_id == s, white[pl.ds(picked[0, s], 1), :], source)
    for out, (d, first, size, with_source) in zip(outs, layout):
        rows = []
        for q in range(2):
            owner = jnp.bitwise_xor(chip, d) * 2 + jnp.bitwise_xor(core, q)
            rows.append(white[pl.ds(pl.multiple_of(owner * shared + first, 8), size), :])
        if with_source:
            rows.append(source)
        out[...] = jnp.concatenate(rows, axis=0).astype(BF16)
    loads[-1].wait()


def pack_kernel(starts, sources, *refs):
    ins, out = refs[:-1], refs[-1]
    parts = [ref[...].astype(F32)[start : start + sources] for ref, start in zip(ins, starts)]
    spare = out.shape[0] - len(ins) * sources
    if spare:
        parts.append(jnp.zeros((spare, WIDTH), F32))
    out[...] = jnp.concatenate(parts, axis=0).astype(BF16)


def gather_kernel(sizes, *refs):
    ins, out = refs[:-1], refs[-1]
    count = len(sizes)
    parts = [ref[...].astype(F32)[n : 2 * n] for ref, n in zip(ins, sizes)]
    parts += [ref[...].astype(F32) for ref in ins[count:]]
    out[...] = jnp.concatenate(parts, axis=0).astype(BF16)


def cross_sums(count, windows, sources, size, src, rec, put):
    block = src.shape[0] // count
    step = 16 if size % 16 == 0 else 8
    for b in range(count):
        for s in range(sources):
            for g in range(0, size, step):
                totals = [0.0] * 4
                for w in range(windows):
                    a = src[pl.ds(b * block + w * sources + s, 1), :]
                    r = rec[pl.ds(w * size + g, step), :]
                    a_re, a_im, a_tail = a[:, :MAIN], a[:, MAIN : 2 * MAIN], a[:, 2 * MAIN :]
                    r_re, r_im = r[:, :MAIN], r[:, MAIN : 2 * MAIN]
                    totals[0] += a_re * r_re + a_im * r_im
                    totals[1] += a_re * r_im - a_im * r_re
                    totals[2] += a_tail * r[:, 2 * MAIN : WIDTH]
                    totals[3] += a_tail * r[:, WIDTH:]
                put(pl.ds((b * sources + s) * size + g, step), jnp.concatenate(totals, axis=1))


def put_receivers(rec, here, value):
    rec[here, :WIDTH] = value
    rec[here, WIDTH:] = pltpu.roll(value[:, 2 * MAIN :], TAIL, 1)


def here_kernel(count, windows, sources, size, places, *refs):
    rec_refs, src_refs = refs[: len(places)], refs[len(places) : len(places) + count]
    lag, half, rec, src, stack = refs[len(places) + count :]
    for ref, (start, n) in zip(rec_refs, places):
        put_receivers(rec, pl.ds(start, n), ref[...].astype(F32)[:n])
    block = src.shape[0] // count
    for b, ref in enumerate(src_refs):
        src[pl.ds(b * block, block), :] = ref[...].astype(F32)
    pairs = half.shape[0]

    def put(here, value):
        high = value.astype(BF16)
        stack[here, :] = high
        stack[pl.ds(pairs + here.start, here.size), :] = (value - high.astype(F32)).astype(BF16)

    cross_sums(count, windows, sources, size, src, rec, put)
    both = jnp.dot(stack[...], lag[: WIDTH + LANES], preferred_element_type=F32)
    low = jnp.dot(stack[:pairs, :], lag[WIDTH + LANES :], preferred_element_type=F32)
    half[...] = both[:pairs] + both[pairs:] + low


def there_kernel(count, windows, sources, size, places, half, other, lag, *refs):
    outs, (rec, src, stack) = refs[:count], refs[count:]
    rows = other[...].astype(F32)
    first = 0
    for start, n in places:
        put_receivers(rec, pl.ds(start, n), rows[first : first + n])
        first += n
    src[...] = rows[first:]

    def put(here, value):
        stack[here, :] = value.astype(BF16)

    cross_sums(count, windows, sources, size, src, rec, put)
    lagged = half[...] + jnp.dot(stack[...], lag[: WIDTH + LANES], preferred_element_type=F32)
    for b in range(count):
        outs[b][...] = lagged[b * sources * size : (b + 1) * sources * size].astype(BF16)


def wanted_kernel(partner, live, _, wanted):
    me = lax.axis_index("chan")
    row_id = lax.broadcasted_iota(jnp.int32, wanted.shape, 0)
    distance = jnp.full(wanted.shape, -1, jnp.int32)
    for p in range(partner.shape[1]):
        value = jnp.where(p < live[0], jnp.bitwise_xor(partner[0, p], me), -1)
        distance = jnp.where(row_id == p, value, distance)
    wanted[...] = distance


def finish_kernel(order, slots, sources, wanted_ref, *refs):
    ins, out = refs[:-1], refs[-1]
    size = out.shape[0]
    for p in range(slots):
        wanted = jnp.broadcast_to(wanted_ref[p : p + 1, :1], (1, 2 * HL))
        value = jnp.zeros((sources * size, 2 * HL), F32)
        for e, ref in zip(order, ins):
            value = jnp.where(wanted == e, ref[...].astype(F32), value)
        for s in range(sources):
            out[:, p, s, :] = value[s * size : (s + 1) * size]


def in_hbm(value):
    return pltpu.with_memory_space_constraint(value, pltpu.HBM)


def call(kernel, out_shape, scratch, spaces, args):
    return pl.pallas_call(
        kernel,
        out_shape=out_shape,
        in_specs=[pl.BlockSpec(memory_space=space) for space in spaces],
        out_specs=jax.tree.map(lambda _: pl.BlockSpec(memory_space=pltpu.VMEM), out_shape),
        scratch_shapes=scratch,
        compiler_params=pltpu.CompilerParams(vmem_limit_bytes=40 * 1024 * 1024),
    )(*args)


def swap(value, axis, size, distance):
    return lax.ppermute(value, axis, [(i, i ^ distance) for i in range(size)])


def local(chans, tms, records, partners, counts, sources):
    channels = records.shape[1]
    picked = sources.shape[1]
    shared = channels // tms
    zs = tms // 2
    size = 2 * shared
    shape = jax.ShapeDtypeStruct
    vmem, smem, hbm = pltpu.VMEM, pltpu.SMEM, pltpu.HBM

    table, band = dft_half(), band_table()
    order = list(reversed(range(zs)))
    first = {d: max(8, shared // 16 * 8) for d in order}
    layout = [(d, 0, first[d], True) for d in order]
    late = [*range(1, zs), 0]
    layout += [(d, first[d], shared - first[d], False) for d in late]
    rows = [2 * n + (SRC_ROWS if src else 0) for _, _, n, src in layout]
    places = [(order.index(d) * shared + row, n) for d, row, n, _ in layout]
    lags = lag_tables(1.0 / math.sqrt(F * tms))
    *sent, lags = call(
        functools.partial(whiten_kernel, layout, shared),
        [shape((n, WIDTH), BF16) for n in rows] + [shape(lags.shape, BF16)],
        [
            pltpu.VMEM((channels, L), BF16),
            pltpu.VMEM(table.shape, BF16),
            pltpu.VMEM(band.shape, BF16),
            pltpu.VMEM((channels, WIDTH), F32),
            pltpu.SMEM(sources.shape, jnp.int32),
            pltpu.SemaphoreType.DMA((5,)),
        ],
        [hbm] * 5,
        (
            *(in_hbm(value) for value in (sources, records)),
            *(in_hbm(jnp.asarray(constant)) for constant in (table, band, lags)),
        ),
    )

    moved = [v if d == 0 else swap(v, "tm", tms, 2 * d) for (d, *_), v in zip(layout, sent)]
    block = -(-zs * picked // SRC_ROWS) * SRC_ROWS
    own = call(
        functools.partial(pack_kernel, [2 * first[d] for d in order], picked),
        shape((block, WIDTH), BF16),
        [],
        [vmem] * zs,
        moved[:zs],
    )
    blocks = list(range(2, chans)) + [1, 0]
    spectra = [own if e == 0 else swap(own, "chan", chans, e) for e in blocks]
    gathered = call(
        functools.partial(gather_kernel, [n for _, _, n, _ in layout]),
        shape((zs * shared + chans * block, WIDTH), BF16),
        [],
        [vmem] * (len(moved) + chans),
        moved + spectra,
    )
    other = swap(gathered, "tm", tms, 1)
    pairs = chans * picked * shared
    scratch = [
        pltpu.VMEM((zs * shared, WIDTH + LANES), F32),
        pltpu.VMEM((chans * block, WIDTH), F32),
    ]
    half = call(
        functools.partial(here_kernel, chans, zs, picked, shared, places),
        shape((pairs, 2 * HL), F32),
        scratch + [pltpu.VMEM((2 * pairs, WIDTH + LANES), BF16)],
        [vmem] * (len(moved) + chans + 1),
        moved + spectra + [lags],
    )
    done = call(
        functools.partial(there_kernel, chans, zs, picked, shared, places),
        [shape((picked * shared, 2 * HL), BF16)] * chans,
        scratch + [pltpu.VMEM((pairs, WIDTH + LANES), BF16)],
        [vmem] * 3,
        (half, other, lags),
    )
    done = dict(zip(blocks, done))
    ways = list(reversed(range(chans)))
    arrived = [done[e] if e == 0 else swap(done[e], "chan", chans, e) for e in ways]
    slots = partners.shape[1]
    wanted = call(
        wanted_kernel,
        shape((-(-slots // 8) * 8, LANES), jnp.int32),
        [],
        [smem, smem, vmem],
        (partners, counts, done[0]),
    )
    result = call(
        functools.partial(finish_kernel, ways, slots, picked),
        shape((shared, slots, picked, 2 * HL), F32),
        [],
        [vmem] * (1 + chans),
        (wanted, *arrived),
    )
    return result[None]


def solution(mesh):
    sizes = dict(mesh.shape)
    return jax.shard_map(
        functools.partial(local, sizes["chan"], sizes["tm"]),
        mesh=mesh,
        in_specs=(P("tm", "chan", None), P("chan", None), P("chan"), P("chan", None)),
        out_specs=P("chan", "tm", None, None, None),
        check_vma=False,
    )
```

```python
import functools
import math

import jax
import jax.numpy as jnp
import ml_dtypes
import numpy as np
from jax import lax
from jax.experimental import pallas as pl
from jax.experimental.pallas import tpu as pltpu
from jax.sharding import PartitionSpec as P

L = 1536
F = 320
HL = 192
SMOOTH = 32
LANES = 128
TAIL = F % LANES
MAIN = F - TAIL
WIDTH = 2 * F
HALF = L // 2
SRC_ROWS = 8
F32 = jnp.float32
BF16 = jnp.bfloat16


def dft_half():
    n = np.arange(HALF)[:, None]
    k = np.arange(F)[None, :] + 1
    angle = (n * k % L).astype(np.float32) * np.float32(2.0 * math.pi / L)
    c, s = np.cos(angle), -np.sin(angle)
    table = np.concatenate([c[:, :MAIN], s[:, :MAIN], c[:, MAIN:], s[:, MAIN:]], axis=1)
    return table.astype(ml_dtypes.bfloat16)


def lag_tables(scale):
    k = np.arange(F)[:, None] + 1
    j = np.arange(2 * HL)[None, :] - HL
    angle = np.mod(k * j, L).astype(np.float32) * np.float32(2.0 * math.pi / L)
    c, s = np.cos(angle) * np.float32(scale), -np.sin(angle) * np.float32(scale)
    table = np.concatenate([c[:MAIN], s[:MAIN], c[MAIN:], c[MAIN:], s[MAIN:], -s[MAIN:]], axis=0)
    high = table.astype(ml_dtypes.bfloat16)
    low = (table - high.astype(np.float32)).astype(ml_dtypes.bfloat16)
    return np.concatenate([high, low], axis=0)


def band_matrix():
    row = lax.broadcasted_iota(jnp.int32, (MAIN + 2 * TAIL, MAIN + 2 * TAIL), 0)
    column = lax.broadcasted_iota(jnp.int32, (MAIN + 2 * TAIL, MAIN + 2 * TAIL), 1)
    column = jnp.where(column >= F, column - TAIL, column)
    centre = jnp.clip(column, SMOOTH, F - 1 - SMOOTH)
    inside = (jnp.abs(row - centre) <= SMOOTH) & (row < F)
    return jnp.where(inside, 1.0, 0.0).astype(BF16)


def whiten(signal, tab, band):
    signal = (signal - jnp.sum(signal, axis=1, keepdims=True) * (1.0 / L)).astype(BF16)
    lane = lax.broadcasted_iota(jnp.int32, (1, WIDTH), 1)
    sign = jnp.where(lane % 2 == 1, 1.0, -1.0).astype(F32)
    spec = jnp.dot(signal[:, :HALF], tab[...], preferred_element_type=F32)
    spec = spec + sign * jnp.dot(signal[:, HALF:], tab[...], preferred_element_type=F32)
    re, im, tail = spec[:, :MAIN], spec[:, MAIN : 2 * MAIN], spec[:, 2 * MAIN :]
    tail_sq = tail * tail
    amp = jnp.sqrt(
        jnp.concatenate([re * re + im * im, tail_sq + pltpu.roll(tail_sq, TAIL, 1)], axis=1)
    )
    high = amp.astype(BF16)
    low = (amp - high.astype(F32)).astype(BF16)
    total = jnp.dot(high, band[...], preferred_element_type=F32) + jnp.dot(
        low, band[...], preferred_element_type=F32
    )
    factor = 1.0 / (total * (1.0 / (2 * SMOOTH + 1)) + 1e-06)
    return re * factor[:, :MAIN], im * factor[:, :MAIN], tail * factor[:, MAIN:]


def keep(ref, here, parts):
    ref[here, :MAIN], ref[here, MAIN : 2 * MAIN], ref[here, 2 * MAIN :] = parts


def whiten_kernel(layout, shared, src_hbm, rec_hbm, tab_hbm, lag_hbm, *rest):
    outs = rest[: len(layout)]
    lag, rec, tab, band, white, picked, sem = rest[len(layout) :]
    loads = [
        pltpu.make_async_copy(*pair, sem.at[i])
        for i, pair in enumerate(
            [
                (rec_hbm.at[0], rec),
                (tab_hbm, tab),
                (src_hbm, picked),
                (lag_hbm, lag),
            ]
        )
    ]
    for load in loads:
        load.start()
    band[...] = band_matrix()
    loads[0].wait()
    signal = rec[...].astype(F32)
    for load in loads[1:-1]:
        load.wait()
    keep(white, slice(None), whiten(signal, tab, band))
    place = lax.axis_index("tm")
    chip, core = place // 2, lax.rem(place, 2)
    row_id = lax.broadcasted_iota(jnp.int32, (SRC_ROWS, WIDTH), 0)
    source = jnp.zeros((SRC_ROWS, WIDTH), F32)
    for s in range(picked.shape[1]):
        source = jnp.where(row_id == s, white[pl.ds(picked[0, s], 1), :], source)
    for out, (d, first, size, with_source) in zip(outs, layout):
        rows = []
        for q in range(2):
            owner = jnp.bitwise_xor(chip, d) * 2 + jnp.bitwise_xor(core, q)
            rows.append(white[pl.ds(pl.multiple_of(owner * shared + first, 8), size), :])
        if with_source:
            rows.append(source)
        out[...] = jnp.concatenate(rows, axis=0).astype(BF16)
    loads[-1].wait()


def pack_kernel(starts, sources, *refs):
    ins, out = refs[:-1], refs[-1]
    parts = [ref[...].astype(F32)[start : start + sources] for ref, start in zip(ins, starts)]
    spare = out.shape[0] - len(ins) * sources
    if spare:
        parts.append(jnp.zeros((spare, WIDTH), F32))
    out[...] = jnp.concatenate(parts, axis=0).astype(BF16)


def gather_kernel(sizes, *refs):
    ins, out = refs[:-1], refs[-1]
    count = len(sizes)
    parts = [ref[...].astype(F32)[n : 2 * n] for ref, n in zip(ins, sizes)]
    parts += [ref[...].astype(F32) for ref in ins[count:]]
    out[...] = jnp.concatenate(parts, axis=0).astype(BF16)


def cross_sums(count, windows, sources, size, src, rec, put):
    block = src.shape[0] // count
    step = 16 if size % 16 == 0 else 8
    for b in range(count):
        for s in range(sources):
            for g in range(0, size, step):
                totals = [0.0] * 4
                for w in range(windows):
                    a = src[pl.ds(b * block + w * sources + s, 1), :]
                    r = rec[pl.ds(w * size + g, step), :]
                    a_re, a_im, a_tail = a[:, :MAIN], a[:, MAIN : 2 * MAIN], a[:, 2 * MAIN :]
                    r_re, r_im = r[:, :MAIN], r[:, MAIN : 2 * MAIN]
                    totals[0] += a_re * r_re + a_im * r_im
                    totals[1] += a_re * r_im - a_im * r_re
                    totals[2] += a_tail * r[:, 2 * MAIN : WIDTH]
                    totals[3] += a_tail * r[:, WIDTH:]
                put(pl.ds((b * sources + s) * size + g, step), jnp.concatenate(totals, axis=1))


def put_receivers(rec, here, value):
    rec[here, :WIDTH] = value
    rec[here, WIDTH:] = pltpu.roll(value[:, 2 * MAIN :], TAIL, 1)


def here_kernel(count, windows, sources, size, places, *refs):
    rec_refs, src_refs = refs[: len(places)], refs[len(places) : len(places) + count]
    lag, half, rec, src, stack = refs[len(places) + count :]
    for ref, (start, n) in zip(rec_refs, places):
        put_receivers(rec, pl.ds(start, n), ref[...].astype(F32)[:n])
    block = src.shape[0] // count
    for b, ref in enumerate(src_refs):
        src[pl.ds(b * block, block), :] = ref[...].astype(F32)
    pairs = half.shape[0]

    def put(here, value):
        high = value.astype(BF16)
        stack[here, :] = high
        stack[pl.ds(pairs + here.start, here.size), :] = (value - high.astype(F32)).astype(BF16)

    cross_sums(count, windows, sources, size, src, rec, put)
    both = jnp.dot(stack[...], lag[: WIDTH + LANES], preferred_element_type=F32)
    low = jnp.dot(stack[:pairs, :], lag[WIDTH + LANES :], preferred_element_type=F32)
    half[...] = both[:pairs] + both[pairs:] + low


def there_kernel(count, windows, sources, size, places, half, other, lag, *refs):
    outs, (rec, src, stack) = refs[:count], refs[count:]
    rows = other[...].astype(F32)
    first = 0
    for start, n in places:
        put_receivers(rec, pl.ds(start, n), rows[first : first + n])
        first += n
    src[...] = rows[first:]

    def put(here, value):
        stack[here, :] = value.astype(BF16)

    cross_sums(count, windows, sources, size, src, rec, put)
    lagged = half[...] + jnp.dot(stack[...], lag[: WIDTH + LANES], preferred_element_type=F32)
    for b in range(count):
        outs[b][...] = lagged[b * sources * size : (b + 1) * sources * size].astype(BF16)


def wanted_kernel(partner, live, _, wanted):
    me = lax.axis_index("chan")
    row_id = lax.broadcasted_iota(jnp.int32, wanted.shape, 0)
    distance = jnp.full(wanted.shape, -1, jnp.int32)
    for p in range(partner.shape[1]):
        value = jnp.where(p < live[0], jnp.bitwise_xor(partner[0, p], me), -1)
        distance = jnp.where(row_id == p, value, distance)
    wanted[...] = distance


def finish_kernel(order, slots, sources, wanted_ref, *refs):
    ins, out, buffer, sem = refs[:-3], refs[-3], refs[-2], refs[-1]
    size = out.shape[0]
    copies = []
    for p in range(slots):
        wanted = jnp.broadcast_to(wanted_ref[p : p + 1, :1], (1, 2 * HL))
        for s in range(sources):
            value = jnp.zeros((size, 2 * HL), F32)
            for e, ref in zip(order, ins):
                value = jnp.where(wanted == e, ref[s * size : (s + 1) * size, :].astype(F32), value)
            buffer[p, :, s, :] = value
        copies.append(pltpu.make_async_copy(buffer.at[p], out.at[:, p], sem.at[p]))
        copies[-1].start()
    for copy in copies:
        copy.wait()


def in_hbm(value):
    return pltpu.with_memory_space_constraint(value, pltpu.HBM)


def call(kernel, out_shape, scratch, spaces, args, out_space=pltpu.VMEM):
    return pl.pallas_call(
        kernel,
        out_shape=out_shape,
        in_specs=[pl.BlockSpec(memory_space=space) for space in spaces],
        out_specs=jax.tree.map(lambda _: pl.BlockSpec(memory_space=out_space), out_shape),
        scratch_shapes=scratch,
        compiler_params=pltpu.CompilerParams(vmem_limit_bytes=40 * 1024 * 1024),
    )(*args)


def swap(value, axis, size, distance):
    return lax.ppermute(value, axis, [(i, i ^ distance) for i in range(size)])


def local(chans, tms, records, partners, counts, sources):
    channels = records.shape[1]
    picked = sources.shape[1]
    shared = channels // tms
    zs = tms // 2
    size = 2 * shared
    shape = jax.ShapeDtypeStruct
    vmem, smem, hbm = pltpu.VMEM, pltpu.SMEM, pltpu.HBM

    table = dft_half()
    order = list(reversed(range(zs)))
    first = {d: max(8, shared // 16 * 8) for d in order}
    layout = [(d, 0, first[d], True) for d in order]
    late = [*range(1, zs), 0]
    layout += [(d, first[d], shared - first[d], False) for d in late]
    rows = [2 * n + (SRC_ROWS if src else 0) for _, _, n, src in layout]
    places = [(order.index(d) * shared + row, n) for d, row, n, _ in layout]
    lags = lag_tables(1.0 / math.sqrt(F * tms))
    *sent, lags = call(
        functools.partial(whiten_kernel, layout, shared),
        [shape((n, WIDTH), BF16) for n in rows] + [shape(lags.shape, BF16)],
        [
            pltpu.VMEM((channels, L), BF16),
            pltpu.VMEM(table.shape, BF16),
            pltpu.VMEM((MAIN + 2 * TAIL, MAIN + 2 * TAIL), BF16),
            pltpu.VMEM((channels, WIDTH), F32),
            pltpu.SMEM(sources.shape, jnp.int32),
            pltpu.SemaphoreType.DMA((5,)),
        ],
        [hbm] * 4,
        (
            *(in_hbm(value) for value in (sources, records)),
            *(in_hbm(jnp.asarray(constant)) for constant in (table, lags)),
        ),
    )

    moved = [v if d == 0 else swap(v, "tm", tms, 2 * d) for (d, *_), v in zip(layout, sent)]
    block = -(-zs * picked // SRC_ROWS) * SRC_ROWS
    own = call(
        functools.partial(pack_kernel, [2 * first[d] for d in order], picked),
        shape((block, WIDTH), BF16),
        [],
        [vmem] * zs,
        moved[:zs],
    )
    blocks = list(range(2, chans)) + [1, 0]
    spectra = [own if e == 0 else swap(own, "chan", chans, e) for e in blocks]
    gathered = call(
        functools.partial(gather_kernel, [n for _, _, n, _ in layout]),
        shape((zs * shared + chans * block, WIDTH), BF16),
        [],
        [vmem] * (len(moved) + chans),
        moved + spectra,
    )
    other = swap(gathered, "tm", tms, 1)
    pairs = chans * picked * shared
    scratch = [
        pltpu.VMEM((zs * shared, WIDTH + LANES), F32),
        pltpu.VMEM((chans * block, WIDTH), F32),
    ]
    half = call(
        functools.partial(here_kernel, chans, zs, picked, shared, places),
        shape((pairs, 2 * HL), F32),
        scratch + [pltpu.VMEM((2 * pairs, WIDTH + LANES), BF16)],
        [vmem] * (len(moved) + chans + 1),
        moved + spectra + [lags],
    )
    done = call(
        functools.partial(there_kernel, chans, zs, picked, shared, places),
        [shape((picked * shared, 2 * HL), BF16)] * chans,
        scratch + [pltpu.VMEM((pairs, WIDTH + LANES), BF16)],
        [vmem] * 3,
        (half, other, lags),
    )
    done = dict(zip(blocks, done))
    ways = list(reversed(range(chans)))
    arrived = [done[e] if e == 0 else swap(done[e], "chan", chans, e) for e in ways]
    slots = partners.shape[1]
    wanted = call(
        wanted_kernel,
        shape((-(-slots // 8) * 8, LANES), jnp.int32),
        [],
        [smem, smem, vmem],
        (partners, counts, done[0]),
    )
    result = call(
        functools.partial(finish_kernel, ways, slots, picked),
        shape((shared, slots, picked, 2 * HL), F32),
        [
            pltpu.VMEM((slots, shared, picked, 2 * HL), F32),
            pltpu.SemaphoreType.DMA((slots,)),
        ],
        [vmem] * (1 + chans),
        (wanted, *arrived),
        out_space=hbm,
    )
    return result[None]


def solution(mesh):
    sizes = dict(mesh.shape)
    return jax.shard_map(
        functools.partial(local, sizes["chan"], sizes["tm"]),
        mesh=mesh,
        in_specs=(P("tm", "chan", None), P("chan", None), P("chan"), P("chan", None)),
        out_specs=P("chan", "tm", None, None, None),
        check_vma=False,
    )
```

```python
import functools
import math

import jax
import jax.numpy as jnp
import ml_dtypes
import numpy as np
from jax import lax
from jax.experimental import pallas as pl
from jax.experimental.pallas import tpu as pltpu
from jax.sharding import PartitionSpec as P

L = 1536
F = 320
HL = 192
SMOOTH = 32
LANES = 128
TAIL = F % LANES
MAIN = F - TAIL
WIDTH = 2 * F
HALF = L // 2
SRC_ROWS = 8
PIECES = 1
F32 = jnp.float32
BF16 = jnp.bfloat16


def dft_half():
    n = np.arange(HALF)[:, None]
    k = np.arange(F)[None, :] + 1
    angle = (n * k % L).astype(np.float32) * np.float32(2.0 * math.pi / L)
    c, s = np.cos(angle), -np.sin(angle)
    table = np.concatenate([c[:, :MAIN], s[:, :MAIN], c[:, MAIN:], s[:, MAIN:]], axis=1)
    return table.astype(ml_dtypes.bfloat16)


def lag_tables(scale):
    k = np.arange(F)[:, None] + 1
    j = np.arange(2 * HL)[None, :] - HL
    angle = np.mod(k * j, L).astype(np.float32) * np.float32(2.0 * math.pi / L)
    c, s = np.cos(angle) * np.float32(scale), -np.sin(angle) * np.float32(scale)
    table = np.concatenate([c[:MAIN], s[:MAIN], c[MAIN:], c[MAIN:], s[MAIN:], -s[MAIN:]], axis=0)
    high = table.astype(ml_dtypes.bfloat16)
    low = (table - high.astype(np.float32)).astype(ml_dtypes.bfloat16)
    return np.concatenate([high, low], axis=0)


def band_matrix():
    row = lax.broadcasted_iota(jnp.int32, (MAIN + 2 * TAIL, MAIN + 2 * TAIL), 0)
    column = lax.broadcasted_iota(jnp.int32, (MAIN + 2 * TAIL, MAIN + 2 * TAIL), 1)
    column = jnp.where(column >= F, column - TAIL, column)
    centre = jnp.clip(column, SMOOTH, F - 1 - SMOOTH)
    inside = (jnp.abs(row - centre) <= SMOOTH) & (row < F)
    return jnp.where(inside, 1.0, 0.0).astype(BF16)


def whiten(signal, tab, band):
    lane = lax.broadcasted_iota(jnp.int32, (1, WIDTH), 1)
    sign = jnp.where(lane % 2 == 1, 1.0, -1.0).astype(F32)
    spec = jnp.dot(signal[:, :HALF], tab[...], preferred_element_type=F32)
    spec = spec + sign * jnp.dot(signal[:, HALF:], tab[...], preferred_element_type=F32)
    re, im, tail = spec[:, :MAIN], spec[:, MAIN : 2 * MAIN], spec[:, 2 * MAIN :]
    tail_sq = tail * tail
    amp = jnp.sqrt(
        jnp.concatenate([re * re + im * im, tail_sq + pltpu.roll(tail_sq, TAIL, 1)], axis=1)
    )
    high = amp.astype(BF16)
    low = (amp - high.astype(F32)).astype(BF16)
    total = jnp.dot(high, band[...], preferred_element_type=F32) + jnp.dot(
        low, band[...], preferred_element_type=F32
    )
    factor = 1.0 / (total * (1.0 / (2 * SMOOTH + 1)) + 1e-06)
    return re * factor[:, :MAIN], im * factor[:, :MAIN], tail * factor[:, MAIN:]


def keep(ref, here, parts):
    ref[here, :MAIN], ref[here, MAIN : 2 * MAIN], ref[here, 2 * MAIN :] = parts


def whiten_kernel(layout, shared, src_hbm, rec_hbm, tab_hbm, lag_hbm, *rest):
    outs = rest[: len(layout)]
    lag, rec, tab, band, white, picked, sem = rest[len(layout) :]
    step = rec.shape[0] // PIECES
    pieces = [pl.ds(i * step, step) for i in range(PIECES)]
    loads = [
        pltpu.make_async_copy(*pair, sem.at[i])
        for i, pair in enumerate(
            [
                *[(rec_hbm.at[0, here], rec.at[here]) for here in pieces],
                (tab_hbm, tab),
                (src_hbm, picked),
                (lag_hbm, lag),
            ]
        )
    ]
    for load in loads:
        load.start()
    band[...] = band_matrix()
    for here, load in zip(pieces, loads):
        load.wait()
        signal = rec[here, :].astype(F32)
        mean = jnp.sum(signal, axis=1, keepdims=True) * (1.0 / L)
        rec[here, :] = (signal - mean).astype(BF16)
    for load in loads[PIECES:-1]:
        load.wait()
    keep(white, slice(None), whiten(rec[...], tab, band))
    place = lax.axis_index("tm")
    chip, core = place // 2, lax.rem(place, 2)
    row_id = lax.broadcasted_iota(jnp.int32, (SRC_ROWS, WIDTH), 0)
    source = jnp.zeros((SRC_ROWS, WIDTH), F32)
    for s in range(picked.shape[1]):
        source = jnp.where(row_id == s, white[pl.ds(picked[0, s], 1), :], source)
    for out, (d, first, size, with_source) in zip(outs, layout):
        rows = []
        for q in range(2):
            owner = jnp.bitwise_xor(chip, d) * 2 + jnp.bitwise_xor(core, q)
            rows.append(white[pl.ds(pl.multiple_of(owner * shared + first, 8), size), :])
        if with_source:
            rows.append(source)
        out[...] = jnp.concatenate(rows, axis=0).astype(BF16)
    loads[-1].wait()


def pack_kernel(starts, sources, *refs):
    ins, out = refs[:-1], refs[-1]
    parts = [ref[...].astype(F32)[start : start + sources] for ref, start in zip(ins, starts)]
    spare = out.shape[0] - len(ins) * sources
    if spare:
        parts.append(jnp.zeros((spare, WIDTH), F32))
    out[...] = jnp.concatenate(parts, axis=0).astype(BF16)


def gather_kernel(sizes, *refs):
    ins, out = refs[:-1], refs[-1]
    count = len(sizes)
    parts = [ref[...].astype(F32)[n : 2 * n] for ref, n in zip(ins, sizes)]
    parts += [ref[...].astype(F32) for ref in ins[count:]]
    out[...] = jnp.concatenate(parts, axis=0).astype(BF16)


def cross_sums(count, windows, sources, size, src, rec, put, blocks=None):
    block = src.shape[0] // count
    step = 16 if size % 16 == 0 else 8
    for b in blocks or range(count):
        for s in range(sources):
            for g in range(0, size, step):
                totals = [0.0] * 4
                for w in range(windows):
                    a = src[pl.ds(b * block + w * sources + s, 1), :]
                    r = rec[pl.ds(w * size + g, step), :]
                    a_re, a_im, a_tail = a[:, :MAIN], a[:, MAIN : 2 * MAIN], a[:, 2 * MAIN :]
                    r_re, r_im = r[:, :MAIN], r[:, MAIN : 2 * MAIN]
                    totals[0] += a_re * r_re + a_im * r_im
                    totals[1] += a_re * r_im - a_im * r_re
                    totals[2] += a_tail * r[:, 2 * MAIN : WIDTH]
                    totals[3] += a_tail * r[:, WIDTH:]
                put(pl.ds((b * sources + s) * size + g, step), jnp.concatenate(totals, axis=1))


def put_receivers(rec, here, value):
    rec[here, :WIDTH] = value
    rec[here, WIDTH:] = pltpu.roll(value[:, 2 * MAIN :], TAIL, 1)


def here_kernel(count, windows, sources, size, places, *refs):
    rec_refs, src_refs = refs[: len(places)], refs[len(places) : len(places) + count]
    lag, half, rec, src, stack = refs[len(places) + count :]
    for ref, (start, n) in zip(rec_refs, places):
        put_receivers(rec, pl.ds(start, n), ref[...].astype(F32)[:n])
    block = src.shape[0] // count
    for b, ref in enumerate(src_refs):
        src[pl.ds(b * block, block), :] = ref[...].astype(F32)
    pairs = half.shape[0]

    def put(here, value):
        high = value.astype(BF16)
        stack[here, :] = high
        stack[pl.ds(pairs + here.start, here.size), :] = (value - high.astype(F32)).astype(BF16)

    cross_sums(count, windows, sources, size, src, rec, put)
    both = jnp.dot(stack[...], lag[: WIDTH + LANES], preferred_element_type=F32)
    low = jnp.dot(stack[:pairs, :], lag[WIDTH + LANES :], preferred_element_type=F32)
    half[...] = both[:pairs] + both[pairs:] + low


def there_kernel(travel, windows, sources, size, places, half, other, lag, *refs):
    outs, (rec, src, stack) = refs[: len(travel)], refs[len(travel) :]
    rows = other[...].astype(F32)
    first = 0
    for start, n in places:
        put_receivers(rec, pl.ds(start, n), rows[first : first + n])
        first += n
    src[...] = rows[first:]
    lag_sums(travel, windows, sources, size, half, src, rec, lag, stack, outs)


def stay_kernel(travel, windows, sources, size, half, rec, src, lag, _, out, stack):
    lag_sums(travel, windows, sources, size, half, src, rec, lag, stack, [out])


def lag_sums(blocks, windows, sources, size, half, src, rec, lag, stack, outs):
    pairs = sources * size
    count = half.shape[0] // pairs
    for i, b in enumerate(blocks):

        def put(here, value, i=i, b=b):
            stack[pl.ds((i - b) * pairs + here.start, here.size), :] = value.astype(BF16)

        cross_sums(count, windows, sources, size, src, rec, put, [b])
    lagged = jnp.dot(stack[...], lag[: WIDTH + LANES], preferred_element_type=F32)
    for i, (b, out) in enumerate(zip(blocks, outs)):
        value = lagged[i * pairs : (i + 1) * pairs] + half[pl.ds(b * pairs, pairs), :]
        out[...] = value.astype(BF16)


def wanted_kernel(partner, live, _, wanted):
    me = lax.axis_index("chan")
    row_id = lax.broadcasted_iota(jnp.int32, wanted.shape, 0)
    distance = jnp.full(wanted.shape, -1, jnp.int32)
    for p in range(partner.shape[1]):
        value = jnp.where(p < live[0], jnp.bitwise_xor(partner[0, p], me), -1)
        distance = jnp.where(row_id == p, value, distance)
    wanted[...] = distance


def finish_kernel(order, slots, sources, wanted_ref, *refs):
    ins, out, buffer, sem = refs[:-3], refs[-3], refs[-2], refs[-1]
    size = out.shape[0]
    copies = []
    for p in range(slots):
        wanted = jnp.broadcast_to(wanted_ref[p : p + 1, :1], (1, 2 * HL))
        for s in range(sources):
            value = jnp.zeros((size, 2 * HL), F32)
            for e, ref in zip(order, ins):
                value = jnp.where(wanted == e, ref[s * size : (s + 1) * size, :].astype(F32), value)
            buffer[p, :, s, :] = value
        copies.append(pltpu.make_async_copy(buffer.at[p], out.at[:, p], sem.at[p]))
        copies[-1].start()
    for copy in copies:
        copy.wait()


def in_hbm(value):
    return pltpu.with_memory_space_constraint(value, pltpu.HBM)


def call(kernel, out_shape, scratch, spaces, args, out_space=pltpu.VMEM):
    return pl.pallas_call(
        kernel,
        out_shape=out_shape,
        in_specs=[pl.BlockSpec(memory_space=space) for space in spaces],
        out_specs=jax.tree.map(lambda _: pl.BlockSpec(memory_space=out_space), out_shape),
        scratch_shapes=scratch,
        compiler_params=pltpu.CompilerParams(vmem_limit_bytes=40 * 1024 * 1024),
    )(*args)


def swap(value, axis, size, distance):
    return lax.ppermute(value, axis, [(i, i ^ distance) for i in range(size)])


def local(chans, tms, records, partners, counts, sources):
    channels = records.shape[1]
    picked = sources.shape[1]
    shared = channels // tms
    zs = tms // 2
    size = 2 * shared
    shape = jax.ShapeDtypeStruct
    vmem, smem, hbm = pltpu.VMEM, pltpu.SMEM, pltpu.HBM

    table = dft_half()
    order = list(reversed(range(zs)))
    first = {d: max(8, shared // 16 * 8) for d in order}
    layout = [(d, 0, first[d], True) for d in order]
    late = [*range(1, zs), 0]
    layout += [(d, first[d], shared - first[d], False) for d in late]
    rows = [2 * n + (SRC_ROWS if src else 0) for _, _, n, src in layout]
    places = [(order.index(d) * shared + row, n) for d, row, n, _ in layout]
    lags = lag_tables(1.0 / math.sqrt(F * tms))
    *sent, lags = call(
        functools.partial(whiten_kernel, layout, shared),
        [shape((n, WIDTH), BF16) for n in rows] + [shape(lags.shape, BF16)],
        [
            pltpu.VMEM((channels, L), BF16),
            pltpu.VMEM(table.shape, BF16),
            pltpu.VMEM((MAIN + 2 * TAIL, MAIN + 2 * TAIL), BF16),
            pltpu.VMEM((channels, WIDTH), F32),
            pltpu.SMEM(sources.shape, jnp.int32),
            pltpu.SemaphoreType.DMA((3 + PIECES,)),
        ],
        [hbm] * 4,
        (
            *(in_hbm(value) for value in (sources, records)),
            *(in_hbm(jnp.asarray(constant)) for constant in (table, lags)),
        ),
    )

    moved = [v if d == 0 else swap(v, "tm", tms, 2 * d) for (d, *_), v in zip(layout, sent)]
    block = -(-zs * picked // SRC_ROWS) * SRC_ROWS
    own = call(
        functools.partial(pack_kernel, [2 * first[d] for d in order], picked),
        shape((block, WIDTH), BF16),
        [],
        [vmem] * zs,
        moved[:zs],
    )
    blocks = list(range(2, chans)) + [1, 0]
    spectra = [own if e == 0 else swap(own, "chan", chans, e) for e in blocks]
    gathered = call(
        functools.partial(gather_kernel, [n for _, _, n, _ in layout]),
        shape((zs * shared + chans * block, WIDTH), BF16),
        [],
        [vmem] * (len(moved) + chans),
        moved + spectra,
    )
    other = swap(gathered, "tm", tms, 1)
    pairs = chans * picked * shared
    scratch = [
        pltpu.VMEM((zs * shared, WIDTH + LANES), F32),
        pltpu.VMEM((chans * block, WIDTH), F32),
    ]
    half = call(
        functools.partial(here_kernel, chans, zs, picked, shared, places),
        shape((pairs, 2 * HL), F32),
        scratch + [pltpu.VMEM((2 * pairs, WIDTH + LANES), BF16)],
        [vmem] * (len(moved) + chans + 1),
        moved + spectra + [lags],
    )
    travel = [i for i, e in enumerate(blocks) if e]
    results = [shape((picked * shared, 2 * HL), BF16)] * len(travel)
    kept = [shape((zs * shared, WIDTH + LANES), F32), shape((chans * block, WIDTH), F32)]
    *done, rec, src = call(
        functools.partial(there_kernel, travel, zs, picked, shared, places),
        results + kept,
        [pltpu.VMEM((len(travel) * picked * shared, WIDTH + LANES), BF16)],
        [vmem] * 3,
        (half, other, lags),
    )
    done = {blocks[i]: value for i, value in zip(travel, done)}
    done[0] = call(
        functools.partial(stay_kernel, [blocks.index(0)], zs, picked, shared),
        shape((picked * shared, 2 * HL), BF16),
        [pltpu.VMEM((picked * shared, WIDTH + LANES), BF16)],
        [vmem] * 5,
        (half, rec, src, lags, done[1]),
    )
    ways = list(reversed(range(chans)))
    arrived = [done[e] if e == 0 else swap(done[e], "chan", chans, e) for e in ways]
    slots = partners.shape[1]
    wanted = call(
        wanted_kernel,
        shape((-(-slots // 8) * 8, LANES), jnp.int32),
        [],
        [smem, smem, vmem],
        (partners, counts, done[1]),
    )
    result = call(
        functools.partial(finish_kernel, ways, slots, picked),
        shape((shared, slots, picked, 2 * HL), F32),
        [
            pltpu.VMEM((slots, shared, picked, 2 * HL), F32),
            pltpu.SemaphoreType.DMA((slots,)),
        ],
        [vmem] * (1 + chans),
        (wanted, *arrived),
        out_space=hbm,
    )
    return result[None]


def solution(mesh):
    sizes = dict(mesh.shape)
    return jax.shard_map(
        functools.partial(local, sizes["chan"], sizes["tm"]),
        mesh=mesh,
        in_specs=(P("tm", "chan", None), P("chan", None), P("chan"), P("chan", None)),
        out_specs=P("chan", "tm", None, None, None),
        check_vma=False,
    )
```

```python
import functools
import math

import jax
import jax.numpy as jnp
import ml_dtypes
import numpy as np
from jax import lax
from jax.experimental import pallas as pl
from jax.experimental.pallas import tpu as pltpu
from jax.sharding import PartitionSpec as P

L = 1536
F = 320
HL = 192
SMOOTH = 32
LANES = 128
TAIL = F % LANES
MAIN = F - TAIL
WIDTH = 2 * F
HALF = L // 2
SRC_ROWS = 8
PIECES = 1
F32 = jnp.float32
BF16 = jnp.bfloat16


def dft_half():
    n = np.arange(HALF)[:, None]
    k = np.arange(F)[None, :] + 1
    angle = (n * k % L).astype(np.float32) * np.float32(2.0 * math.pi / L)
    c, s = np.cos(angle), -np.sin(angle)
    table = np.concatenate([c[:, :MAIN], s[:, :MAIN], c[:, MAIN:], s[:, MAIN:]], axis=1)
    return table.astype(ml_dtypes.bfloat16)


def lag_tables(scale):
    k = np.arange(F)[:, None] + 1
    j = np.arange(2 * HL)[None, :] - HL
    angle = np.mod(k * j, L).astype(np.float32) * np.float32(2.0 * math.pi / L)
    c, s = np.cos(angle) * np.float32(scale), -np.sin(angle) * np.float32(scale)
    table = np.concatenate([c[:MAIN], s[:MAIN], c[MAIN:], c[MAIN:], s[MAIN:], -s[MAIN:]], axis=0)
    high = table.astype(ml_dtypes.bfloat16)
    low = (table - high.astype(np.float32)).astype(ml_dtypes.bfloat16)
    return np.concatenate([high, low], axis=0)


def band_matrix():
    row = lax.broadcasted_iota(jnp.int32, (MAIN + 2 * TAIL, MAIN + 2 * TAIL), 0)
    column = lax.broadcasted_iota(jnp.int32, (MAIN + 2 * TAIL, MAIN + 2 * TAIL), 1)
    column = jnp.where(column >= F, column - TAIL, column)
    centre = jnp.clip(column, SMOOTH, F - 1 - SMOOTH)
    inside = (jnp.abs(row - centre) <= SMOOTH) & (row < F)
    return jnp.where(inside, 1.0, 0.0).astype(BF16)


def whiten(signal, tab, band):
    lane = lax.broadcasted_iota(jnp.int32, (1, WIDTH), 1)
    sign = jnp.where(lane % 2 == 1, 1.0, -1.0).astype(F32)
    spec = jnp.dot(signal[:, :HALF], tab[...], preferred_element_type=F32)
    spec = spec + sign * jnp.dot(signal[:, HALF:], tab[...], preferred_element_type=F32)
    re, im, tail = spec[:, :MAIN], spec[:, MAIN : 2 * MAIN], spec[:, 2 * MAIN :]
    tail_sq = tail * tail
    amp = jnp.sqrt(
        jnp.concatenate([re * re + im * im, tail_sq + pltpu.roll(tail_sq, TAIL, 1)], axis=1)
    )
    high = amp.astype(BF16)
    low = (amp - high.astype(F32)).astype(BF16)
    total = jnp.dot(high, band[...], preferred_element_type=F32) + jnp.dot(
        low, band[...], preferred_element_type=F32
    )
    factor = 1.0 / (total * (1.0 / (2 * SMOOTH + 1)) + 1e-06)
    return re * factor[:, :MAIN], im * factor[:, :MAIN], tail * factor[:, MAIN:]


def keep(ref, here, parts):
    ref[here, :MAIN], ref[here, MAIN : 2 * MAIN], ref[here, 2 * MAIN :] = parts


def whiten_kernel(layout, shared, src_hbm, rec_hbm, tab_hbm, lag_hbm, *rest):
    outs = rest[: len(layout)]
    lag, rec, tab, band, white, picked, sem = rest[len(layout) :]
    step = rec.shape[0] // PIECES
    pieces = [pl.ds(i * step, step) for i in range(PIECES)]
    loads = [
        pltpu.make_async_copy(*pair, sem.at[i])
        for i, pair in enumerate(
            [
                *[(rec_hbm.at[0, here], rec.at[here]) for here in pieces],
                (tab_hbm, tab),
                (src_hbm, picked),
                (lag_hbm, lag),
            ]
        )
    ]
    for load in loads:
        load.start()
    band[...] = band_matrix()
    for here, load in zip(pieces, loads):
        load.wait()
        signal = rec[here, :].astype(F32)
        mean = jnp.sum(signal, axis=1, keepdims=True) * (1.0 / L)
        rec[here, :] = (signal - mean).astype(BF16)
    for load in loads[PIECES:-1]:
        load.wait()
    keep(white, slice(None), whiten(rec[...], tab, band))
    place = lax.axis_index("tm")
    chip, core = place // 2, lax.rem(place, 2)
    row_id = lax.broadcasted_iota(jnp.int32, (SRC_ROWS, WIDTH), 0)
    source = jnp.zeros((SRC_ROWS, WIDTH), F32)
    for s in range(picked.shape[1]):
        source = jnp.where(row_id == s, white[pl.ds(picked[0, s], 1), :], source)
    for out, (d, first, size, with_source) in zip(outs, layout):
        rows = []
        for q in range(2):
            owner = jnp.bitwise_xor(chip, d) * 2 + jnp.bitwise_xor(core, q)
            rows.append(white[pl.ds(pl.multiple_of(owner * shared + first, 8), size), :])
        if with_source:
            rows.append(source)
        out[...] = jnp.concatenate(rows, axis=0).astype(BF16)
    loads[-1].wait()


def pack_kernel(starts, sources, *refs):
    ins, out = refs[:-1], refs[-1]
    parts = [ref[...].astype(F32)[start : start + sources] for ref, start in zip(ins, starts)]
    spare = out.shape[0] - len(ins) * sources
    if spare:
        parts.append(jnp.zeros((spare, WIDTH), F32))
    out[...] = jnp.concatenate(parts, axis=0).astype(BF16)


def gather_kernel(sizes, *refs):
    ins, out = refs[:-1], refs[-1]
    count = len(sizes)
    parts = [ref[...].astype(F32)[n : 2 * n] for ref, n in zip(ins, sizes)]
    parts += [ref[...].astype(F32) for ref in ins[count:]]
    out[...] = jnp.concatenate(parts, axis=0).astype(BF16)


def cross_sums(count, windows, sources, size, src, rec, put, blocks=None):
    block = src.shape[0] // count
    step = 16 if size % 16 == 0 else 8
    for b in blocks or range(count):
        for s in range(sources):
            for g in range(0, size, step):
                totals = [0.0] * 4
                for w in range(windows):
                    a = src[pl.ds(b * block + w * sources + s, 1), :]
                    r = rec[pl.ds(w * size + g, step), :]
                    a_re, a_im, a_tail = a[:, :MAIN], a[:, MAIN : 2 * MAIN], a[:, 2 * MAIN :]
                    r_re, r_im = r[:, :MAIN], r[:, MAIN : 2 * MAIN]
                    totals[0] += a_re * r_re + a_im * r_im
                    totals[1] += a_re * r_im - a_im * r_re
                    totals[2] += a_tail * r[:, 2 * MAIN : WIDTH]
                    totals[3] += a_tail * r[:, WIDTH:]
                put(pl.ds((b * sources + s) * size + g, step), jnp.concatenate(totals, axis=1))


def put_receivers(rec, here, value):
    rec[here, :WIDTH] = value
    rec[here, WIDTH:] = pltpu.roll(value[:, 2 * MAIN :], TAIL, 1)


def here_kernel(count, windows, sources, size, places, *refs):
    rec_refs, src_refs = refs[: len(places)], refs[len(places) : len(places) + count]
    lag, half, rec, src, stack = refs[len(places) + count :]
    for ref, (start, n) in zip(rec_refs, places):
        put_receivers(rec, pl.ds(start, n), ref[...].astype(F32)[:n])
    block = src.shape[0] // count
    for b, ref in enumerate(src_refs):
        src[pl.ds(b * block, block), :] = ref[...].astype(F32)
    pairs = half.shape[0]

    def put(here, value):
        high = value.astype(BF16)
        stack[here, :] = high
        stack[pl.ds(pairs + here.start, here.size), :] = (value - high.astype(F32)).astype(BF16)

    cross_sums(count, windows, sources, size, src, rec, put)
    both = jnp.dot(stack[...], lag[: WIDTH + LANES], preferred_element_type=F32)
    low = jnp.dot(stack[:pairs, :], lag[WIDTH + LANES :], preferred_element_type=F32)
    half[...] = both[:pairs] + both[pairs:] + low


def there_kernel(travel, windows, sources, size, places, half, other, lag, *refs):
    outs, (rec, src, stack) = refs[: len(travel)], refs[len(travel) :]
    rows = other[...].astype(F32)
    first = 0
    for start, n in places:
        put_receivers(rec, pl.ds(start, n), rows[first : first + n])
        first += n
    src[...] = rows[first:]
    lag_sums(travel, windows, sources, size, half, src, rec, lag, stack, outs)


def stay_kernel(travel, windows, sources, size, half, rec, src, lag, _, out, stack):
    lag_sums(travel, windows, sources, size, half, src, rec, lag, stack, [out])


def lag_sums(blocks, windows, sources, size, half, src, rec, lag, stack, outs):
    pairs = sources * size
    count = half.shape[0] // pairs
    for i, b in enumerate(blocks):

        def put(here, value, i=i, b=b):
            stack[pl.ds((i - b) * pairs + here.start, here.size), :] = value.astype(BF16)

        cross_sums(count, windows, sources, size, src, rec, put, [b])
    lagged = jnp.dot(stack[...], lag[: WIDTH + LANES], preferred_element_type=F32)
    for i, (b, out) in enumerate(zip(blocks, outs)):
        value = lagged[i * pairs : (i + 1) * pairs] + half[pl.ds(b * pairs, pairs), :]
        out[...] = value.astype(BF16)


def wanted_kernel(partner, live, _, wanted):
    me = lax.axis_index("chan")
    row_id = lax.broadcasted_iota(jnp.int32, wanted.shape, 0)
    distance = jnp.full(wanted.shape, -1, jnp.int32)
    for p in range(partner.shape[1]):
        value = jnp.where(p < live[0], jnp.bitwise_xor(partner[0, p], me), -1)
        distance = jnp.where(row_id == p, value, distance)
    wanted[...] = distance


def finish_kernel(order, slots, sources, wanted_ref, *refs):
    ins, out, buffer, sem = refs[:-3], refs[-3], refs[-2], refs[-1]
    size = out.shape[0]
    copies = []
    for p in range(slots):
        wanted = jnp.broadcast_to(wanted_ref[p : p + 1, :1], (1, 2 * HL))
        for s in range(sources):
            value = jnp.zeros((size, 2 * HL), F32)
            for e, ref in zip(order, ins):
                value = jnp.where(wanted == e, ref[s * size : (s + 1) * size, :].astype(F32), value)
            buffer[p, :, s, :] = value
        copies.append(pltpu.make_async_copy(buffer.at[p], out.at[:, p], sem.at[p]))
        copies[-1].start()
    for copy in copies:
        copy.wait()


def in_hbm(value):
    return pltpu.with_memory_space_constraint(value, pltpu.HBM)


def call(kernel, out_shape, scratch, spaces, args, out_space=pltpu.VMEM):
    return pl.pallas_call(
        kernel,
        out_shape=out_shape,
        in_specs=[pl.BlockSpec(memory_space=space) for space in spaces],
        out_specs=jax.tree.map(lambda _: pl.BlockSpec(memory_space=out_space), out_shape),
        scratch_shapes=scratch,
        compiler_params=pltpu.CompilerParams(vmem_limit_bytes=40 * 1024 * 1024),
    )(*args)


def swap(value, axis, size, distance):
    return lax.ppermute(value, axis, [(i, i ^ distance) for i in range(size)])


def local(chans, tms, records, partners, counts, sources):
    channels = records.shape[1]
    picked = sources.shape[1]
    shared = channels // tms
    zs = tms // 2
    size = 2 * shared
    shape = jax.ShapeDtypeStruct
    vmem, smem, hbm = pltpu.VMEM, pltpu.SMEM, pltpu.HBM

    table = dft_half()
    order = list(reversed(range(zs)))
    first = {d: max(8, shared // 16 * 8) for d in order}
    layout = [(d, 0, first[d], True) for d in order]
    late = [*range(1, zs), 0]
    layout += [(d, first[d], shared - first[d], False) for d in late]
    rows = [2 * n + (SRC_ROWS if src else 0) for _, _, n, src in layout]
    places = [(order.index(d) * shared + row, n) for d, row, n, _ in layout]
    lags = lag_tables(1.0 / math.sqrt(F * tms))
    *sent, lags = call(
        functools.partial(whiten_kernel, layout, shared),
        [shape((n, WIDTH), BF16) for n in rows] + [shape(lags.shape, BF16)],
        [
            pltpu.VMEM((channels, L), BF16),
            pltpu.VMEM(table.shape, BF16),
            pltpu.VMEM((MAIN + 2 * TAIL, MAIN + 2 * TAIL), BF16),
            pltpu.VMEM((channels, WIDTH), F32),
            pltpu.SMEM(sources.shape, jnp.int32),
            pltpu.SemaphoreType.DMA((3 + PIECES,)),
        ],
        [hbm] * 4,
        (
            *(in_hbm(value) for value in (sources, records)),
            *(in_hbm(jnp.asarray(constant)) for constant in (table, lags)),
        ),
    )

    moved = [v if d == 0 else swap(v, "tm", tms, 2 * d) for (d, *_), v in zip(layout, sent)]
    block = -(-zs * picked // SRC_ROWS) * SRC_ROWS
    own = call(
        functools.partial(pack_kernel, [2 * first[d] for d in order], picked),
        shape((block, WIDTH), BF16),
        [],
        [vmem] * zs,
        moved[:zs],
    )
    blocks = list(reversed(range(chans)))
    spectra = [own if e == 0 else swap(own, "chan", chans, e) for e in blocks]
    gathered = call(
        functools.partial(gather_kernel, [n for _, _, n, _ in layout]),
        shape((zs * shared + chans * block, WIDTH), BF16),
        [],
        [vmem] * (len(moved) + chans),
        moved + spectra,
    )
    other = swap(gathered, "tm", tms, 1)
    pairs = chans * picked * shared
    scratch = [
        pltpu.VMEM((zs * shared, WIDTH + LANES), F32),
        pltpu.VMEM((chans * block, WIDTH), F32),
    ]
    half = call(
        functools.partial(here_kernel, chans, zs, picked, shared, places),
        shape((pairs, 2 * HL), F32),
        scratch + [pltpu.VMEM((2 * pairs, WIDTH + LANES), BF16)],
        [vmem] * (len(moved) + chans + 1),
        moved + spectra + [lags],
    )
    travel = [i for i, e in enumerate(blocks) if e]
    results = [shape((picked * shared, 2 * HL), BF16)] * len(travel)
    kept = [shape((zs * shared, WIDTH + LANES), F32), shape((chans * block, WIDTH), F32)]
    *done, rec, src = call(
        functools.partial(there_kernel, travel, zs, picked, shared, places),
        results + kept,
        [pltpu.VMEM((len(travel) * picked * shared, WIDTH + LANES), BF16)],
        [vmem] * 3,
        (half, other, lags),
    )
    done = {blocks[i]: value for i, value in zip(travel, done)}
    done[0] = call(
        functools.partial(stay_kernel, [blocks.index(0)], zs, picked, shared),
        shape((picked * shared, 2 * HL), BF16),
        [pltpu.VMEM((picked * shared, WIDTH + LANES), BF16)],
        [vmem] * 5,
        (half, rec, src, lags, done[1]),
    )
    ways = list(reversed(range(chans)))
    arrived = [done[e] if e == 0 else swap(done[e], "chan", chans, e) for e in ways]
    slots = partners.shape[1]
    wanted = call(
        wanted_kernel,
        shape((-(-slots // 8) * 8, LANES), jnp.int32),
        [],
        [smem, smem, vmem],
        (partners, counts, done[1]),
    )
    result = call(
        functools.partial(finish_kernel, ways, slots, picked),
        shape((shared, slots, picked, 2 * HL), F32),
        [
            pltpu.VMEM((slots, shared, picked, 2 * HL), F32),
            pltpu.SemaphoreType.DMA((slots,)),
        ],
        [vmem] * (1 + chans),
        (wanted, *arrived),
        out_space=hbm,
    )
    return result[None]


def solution(mesh):
    sizes = dict(mesh.shape)
    return jax.shard_map(
        functools.partial(local, sizes["chan"], sizes["tm"]),
        mesh=mesh,
        in_specs=(P("tm", "chan", None), P("chan", None), P("chan"), P("chan", None)),
        out_specs=P("chan", "tm", None, None, None),
        check_vma=False,
    )
```

```python
import functools
import math

import jax
import jax.numpy as jnp
import ml_dtypes
import numpy as np
from jax import lax
from jax.experimental import pallas as pl
from jax.experimental.pallas import tpu as pltpu
from jax.sharding import PartitionSpec as P

L = 1536
F = 320
HL = 192
SMOOTH = 32
LANES = 128
TAIL = F % LANES
MAIN = F - TAIL
WIDTH = 2 * F
HALF = L // 2
SRC_ROWS = 8
PIECES = 4
F32 = jnp.float32
BF16 = jnp.bfloat16


def dft_half():
    n = np.arange(HALF)[:, None]
    k = np.arange(F)[None, :] + 1
    angle = (n * k % L).astype(np.float32) * np.float32(2.0 * math.pi / L)
    c, s = np.cos(angle), -np.sin(angle)
    table = np.concatenate([c[:, :MAIN], s[:, :MAIN], c[:, MAIN:], s[:, MAIN:]], axis=1)
    return table.astype(ml_dtypes.bfloat16)


def lag_tables(scale):
    k = np.arange(F)[:, None] + 1
    j = np.arange(2 * HL)[None, :] - HL
    angle = np.mod(k * j, L).astype(np.float32) * np.float32(2.0 * math.pi / L)
    c, s = np.cos(angle) * np.float32(scale), -np.sin(angle) * np.float32(scale)
    table = np.concatenate([c[:MAIN], s[:MAIN], c[MAIN:], c[MAIN:], s[MAIN:], -s[MAIN:]], axis=0)
    high = table.astype(ml_dtypes.bfloat16)
    low = (table - high.astype(np.float32)).astype(ml_dtypes.bfloat16)
    return np.concatenate([high, low], axis=0)


def band_matrix():
    row = lax.broadcasted_iota(jnp.int32, (MAIN + 2 * TAIL, MAIN + 2 * TAIL), 0)
    column = lax.broadcasted_iota(jnp.int32, (MAIN + 2 * TAIL, MAIN + 2 * TAIL), 1)
    column = jnp.where(column >= F, column - TAIL, column)
    centre = jnp.clip(column, SMOOTH, F - 1 - SMOOTH)
    inside = (jnp.abs(row - centre) <= SMOOTH) & (row < F)
    return jnp.where(inside, 1.0, 0.0).astype(BF16)


def whiten(signal, tab, band):
    lane = lax.broadcasted_iota(jnp.int32, (1, WIDTH), 1)
    sign = jnp.where(lane % 2 == 1, 1.0, -1.0).astype(F32)
    spec = jnp.dot(signal[:, :HALF], tab[...], preferred_element_type=F32)
    spec = spec + sign * jnp.dot(signal[:, HALF:], tab[...], preferred_element_type=F32)
    re, im, tail = spec[:, :MAIN], spec[:, MAIN : 2 * MAIN], spec[:, 2 * MAIN :]
    tail_sq = tail * tail
    amp = jnp.sqrt(
        jnp.concatenate([re * re + im * im, tail_sq + pltpu.roll(tail_sq, TAIL, 1)], axis=1)
    )
    high = amp.astype(BF16)
    low = (amp - high.astype(F32)).astype(BF16)
    total = jnp.dot(high, band[...], preferred_element_type=F32) + jnp.dot(
        low, band[...], preferred_element_type=F32
    )
    factor = 1.0 / (total * (1.0 / (2 * SMOOTH + 1)) + 1e-06)
    return re * factor[:, :MAIN], im * factor[:, :MAIN], tail * factor[:, MAIN:]


def keep(ref, here, parts):
    ref[here, :MAIN], ref[here, MAIN : 2 * MAIN], ref[here, 2 * MAIN :] = parts


def whiten_kernel(layout, shared, src_hbm, rec_hbm, tab_hbm, lag_hbm, *rest):
    outs = rest[: len(layout)]
    lag, rec, tab, band, white, picked, sem = rest[len(layout) :]
    step = rec.shape[0] // PIECES
    pieces = [pl.ds(i * step, step) for i in range(PIECES)]
    loads = [
        pltpu.make_async_copy(*pair, sem.at[i])
        for i, pair in enumerate(
            [
                *[(rec_hbm.at[0, here], rec.at[here]) for here in pieces],
                (tab_hbm, tab),
                (src_hbm, picked),
                (lag_hbm, lag),
            ]
        )
    ]
    for load in loads:
        load.start()
    band[...] = band_matrix()
    for here, load in zip(pieces, loads):
        load.wait()
        signal = rec[here, :].astype(F32)
        mean = jnp.sum(signal, axis=1, keepdims=True) * (1.0 / L)
        rec[here, :] = (signal - mean).astype(BF16)
    for load in loads[PIECES:-1]:
        load.wait()
    keep(white, slice(None), whiten(rec[...], tab, band))
    place = lax.axis_index("tm")
    chip, core = place // 2, lax.rem(place, 2)
    row_id = lax.broadcasted_iota(jnp.int32, (SRC_ROWS, WIDTH), 0)
    source = jnp.zeros((SRC_ROWS, WIDTH), F32)
    for s in range(picked.shape[1]):
        source = jnp.where(row_id == s, white[pl.ds(picked[0, s], 1), :], source)
    for out, (d, first, size, with_source) in zip(outs, layout):
        rows = []
        for q in range(2):
            owner = jnp.bitwise_xor(chip, d) * 2 + jnp.bitwise_xor(core, q)
            rows.append(white[pl.ds(pl.multiple_of(owner * shared + first, 8), size), :])
        if with_source:
            rows.append(source)
        out[...] = jnp.concatenate(rows, axis=0).astype(BF16)
    loads[-1].wait()


def pack_kernel(starts, sources, *refs):
    ins, out = refs[:-1], refs[-1]
    parts = [ref[...].astype(F32)[start : start + sources] for ref, start in zip(ins, starts)]
    spare = out.shape[0] - len(ins) * sources
    if spare:
        parts.append(jnp.zeros((spare, WIDTH), F32))
    out[...] = jnp.concatenate(parts, axis=0).astype(BF16)


def gather_kernel(sizes, *refs):
    ins, out = refs[:-1], refs[-1]
    count = len(sizes)
    parts = [ref[...].astype(F32)[n : 2 * n] for ref, n in zip(ins, sizes)]
    parts += [ref[...].astype(F32) for ref in ins[count:]]
    out[...] = jnp.concatenate(parts, axis=0).astype(BF16)


def cross_sums(count, windows, sources, size, src, rec, put, blocks=None):
    block = src.shape[0] // count
    step = 16 if size % 16 == 0 else 8
    for b in blocks or range(count):
        for s in range(sources):
            for g in range(0, size, step):
                totals = [0.0] * 4
                for w in range(windows):
                    a = src[pl.ds(b * block + w * sources + s, 1), :]
                    r = rec[pl.ds(w * size + g, step), :]
                    a_re, a_im, a_tail = a[:, :MAIN], a[:, MAIN : 2 * MAIN], a[:, 2 * MAIN :]
                    r_re, r_im = r[:, :MAIN], r[:, MAIN : 2 * MAIN]
                    totals[0] += a_re * r_re + a_im * r_im
                    totals[1] += a_re * r_im - a_im * r_re
                    totals[2] += a_tail * r[:, 2 * MAIN : WIDTH]
                    totals[3] += a_tail * r[:, WIDTH:]
                put(pl.ds((b * sources + s) * size + g, step), jnp.concatenate(totals, axis=1))


def put_receivers(rec, here, value):
    rec[here, :WIDTH] = value
    rec[here, WIDTH:] = pltpu.roll(value[:, 2 * MAIN :], TAIL, 1)


def here_kernel(count, windows, sources, size, places, *refs):
    rec_refs, src_refs = refs[: len(places)], refs[len(places) : len(places) + count]
    lag, half, rec, src, stack = refs[len(places) + count :]
    for ref, (start, n) in zip(rec_refs, places):
        put_receivers(rec, pl.ds(start, n), ref[...].astype(F32)[:n])
    block = src.shape[0] // count
    for b, ref in enumerate(src_refs):
        src[pl.ds(b * block, block), :] = ref[...].astype(F32)
    pairs = half.shape[0]

    def put(here, value):
        high = value.astype(BF16)
        stack[here, :] = high
        stack[pl.ds(pairs + here.start, here.size), :] = (value - high.astype(F32)).astype(BF16)

    cross_sums(count, windows, sources, size, src, rec, put)
    both = jnp.dot(stack[...], lag[: WIDTH + LANES], preferred_element_type=F32)
    low = jnp.dot(stack[:pairs, :], lag[WIDTH + LANES :], preferred_element_type=F32)
    half[...] = both[:pairs] + both[pairs:] + low


def there_kernel(travel, windows, sources, size, places, half, other, lag, *refs):
    outs, (rec, src, stack) = refs[: len(travel)], refs[len(travel) :]
    rows = other[...].astype(F32)
    first = 0
    for start, n in places:
        put_receivers(rec, pl.ds(start, n), rows[first : first + n])
        first += n
    src[...] = rows[first:]
    lag_sums(travel, windows, sources, size, half, src, rec, lag, stack, outs)


def stay_kernel(travel, windows, sources, size, half, rec, src, lag, _, out, stack):
    lag_sums(travel, windows, sources, size, half, src, rec, lag, stack, [out])


def lag_sums(blocks, windows, sources, size, half, src, rec, lag, stack, outs):
    pairs = sources * size
    count = half.shape[0] // pairs
    for i, b in enumerate(blocks):

        def put(here, value, i=i, b=b):
            stack[pl.ds((i - b) * pairs + here.start, here.size), :] = value.astype(BF16)

        cross_sums(count, windows, sources, size, src, rec, put, [b])
    lagged = jnp.dot(stack[...], lag[: WIDTH + LANES], preferred_element_type=F32)
    for i, (b, out) in enumerate(zip(blocks, outs)):
        value = lagged[i * pairs : (i + 1) * pairs] + half[pl.ds(b * pairs, pairs), :]
        out[...] = value.astype(BF16)


def wanted_kernel(partner, live, _, wanted):
    me = lax.axis_index("chan")
    row_id = lax.broadcasted_iota(jnp.int32, wanted.shape, 0)
    distance = jnp.full(wanted.shape, -1, jnp.int32)
    for p in range(partner.shape[1]):
        value = jnp.where(p < live[0], jnp.bitwise_xor(partner[0, p], me), -1)
        distance = jnp.where(row_id == p, value, distance)
    wanted[...] = distance


def finish_kernel(order, slots, sources, wanted_ref, *refs):
    ins, out, buffer, sem = refs[:-3], refs[-3], refs[-2], refs[-1]
    size = out.shape[0]
    copies = []
    for p in range(slots):
        wanted = jnp.broadcast_to(wanted_ref[p : p + 1, :1], (1, 2 * HL))
        for s in range(sources):
            value = jnp.zeros((size, 2 * HL), F32)
            for e, ref in zip(order, ins):
                value = jnp.where(wanted == e, ref[s * size : (s + 1) * size, :].astype(F32), value)
            buffer[p, :, s, :] = value
        copies.append(pltpu.make_async_copy(buffer.at[p], out.at[:, p], sem.at[p]))
        copies[-1].start()
    for copy in copies:
        copy.wait()


def in_hbm(value):
    return pltpu.with_memory_space_constraint(value, pltpu.HBM)


def call(kernel, out_shape, scratch, spaces, args, out_space=pltpu.VMEM):
    return pl.pallas_call(
        kernel,
        out_shape=out_shape,
        in_specs=[pl.BlockSpec(memory_space=space) for space in spaces],
        out_specs=jax.tree.map(lambda _: pl.BlockSpec(memory_space=out_space), out_shape),
        scratch_shapes=scratch,
        compiler_params=pltpu.CompilerParams(vmem_limit_bytes=40 * 1024 * 1024),
    )(*args)


def swap(value, axis, size, distance):
    return lax.ppermute(value, axis, [(i, i ^ distance) for i in range(size)])


def local(chans, tms, records, partners, counts, sources):
    channels = records.shape[1]
    picked = sources.shape[1]
    shared = channels // tms
    zs = tms // 2
    size = 2 * shared
    shape = jax.ShapeDtypeStruct
    vmem, smem, hbm = pltpu.VMEM, pltpu.SMEM, pltpu.HBM

    table = dft_half()
    order = list(reversed(range(zs)))
    first = {d: max(8, shared // 16 * 8) for d in order}
    layout = [(d, 0, first[d], True) for d in order]
    late = [*range(1, zs), 0]
    layout += [(d, first[d], shared - first[d], False) for d in late]
    rows = [2 * n + (SRC_ROWS if src else 0) for _, _, n, src in layout]
    places = [(order.index(d) * shared + row, n) for d, row, n, _ in layout]
    lags = lag_tables(1.0 / math.sqrt(F * tms))
    *sent, lags = call(
        functools.partial(whiten_kernel, layout, shared),
        [shape((n, WIDTH), BF16) for n in rows] + [shape(lags.shape, BF16)],
        [
            pltpu.VMEM((channels, L), BF16),
            pltpu.VMEM(table.shape, BF16),
            pltpu.VMEM((MAIN + 2 * TAIL, MAIN + 2 * TAIL), BF16),
            pltpu.VMEM((channels, WIDTH), F32),
            pltpu.SMEM(sources.shape, jnp.int32),
            pltpu.SemaphoreType.DMA((3 + PIECES,)),
        ],
        [hbm] * 4,
        (
            *(in_hbm(value) for value in (sources, records)),
            *(in_hbm(jnp.asarray(constant)) for constant in (table, lags)),
        ),
    )

    moved = [v if d == 0 else swap(v, "tm", tms, 2 * d) for (d, *_), v in zip(layout, sent)]
    block = -(-zs * picked // SRC_ROWS) * SRC_ROWS
    own = call(
        functools.partial(pack_kernel, [2 * first[d] for d in order], picked),
        shape((block, WIDTH), BF16),
        [],
        [vmem] * zs,
        moved[:zs],
    )
    blocks = list(reversed(range(chans)))
    spectra = [own if e == 0 else swap(own, "chan", chans, e) for e in blocks]
    gathered = call(
        functools.partial(gather_kernel, [n for _, _, n, _ in layout]),
        shape((zs * shared + chans * block, WIDTH), BF16),
        [],
        [vmem] * (len(moved) + chans),
        moved + spectra,
    )
    other = swap(gathered, "tm", tms, 1)
    pairs = chans * picked * shared
    scratch = [
        pltpu.VMEM((zs * shared, WIDTH + LANES), F32),
        pltpu.VMEM((chans * block, WIDTH), F32),
    ]
    half = call(
        functools.partial(here_kernel, chans, zs, picked, shared, places),
        shape((pairs, 2 * HL), F32),
        scratch + [pltpu.VMEM((2 * pairs, WIDTH + LANES), BF16)],
        [vmem] * (len(moved) + chans + 1),
        moved + spectra + [lags],
    )
    travel = [i for i, e in enumerate(blocks) if e]
    results = [shape((picked * shared, 2 * HL), BF16)] * len(travel)
    kept = [shape((zs * shared, WIDTH + LANES), F32), shape((chans * block, WIDTH), F32)]
    *done, rec, src = call(
        functools.partial(there_kernel, travel, zs, picked, shared, places),
        results + kept,
        [pltpu.VMEM((len(travel) * picked * shared, WIDTH + LANES), BF16)],
        [vmem] * 3,
        (half, other, lags),
    )
    done = {blocks[i]: value for i, value in zip(travel, done)}
    done[0] = call(
        functools.partial(stay_kernel, [blocks.index(0)], zs, picked, shared),
        shape((picked * shared, 2 * HL), BF16),
        [pltpu.VMEM((picked * shared, WIDTH + LANES), BF16)],
        [vmem] * 5,
        (half, rec, src, lags, done[1]),
    )
    ways = list(reversed(range(chans)))
    arrived = [done[e] if e == 0 else swap(done[e], "chan", chans, e) for e in ways]
    slots = partners.shape[1]
    wanted = call(
        wanted_kernel,
        shape((-(-slots // 8) * 8, LANES), jnp.int32),
        [],
        [smem, smem, vmem],
        (partners, counts, done[1]),
    )
    result = call(
        functools.partial(finish_kernel, ways, slots, picked),
        shape((shared, slots, picked, 2 * HL), F32),
        [
            pltpu.VMEM((slots, shared, picked, 2 * HL), F32),
            pltpu.SemaphoreType.DMA((slots,)),
        ],
        [vmem] * (1 + chans),
        (wanted, *arrived),
        out_space=hbm,
    )
    return result[None]


def solution(mesh):
    sizes = dict(mesh.shape)
    return jax.shard_map(
        functools.partial(local, sizes["chan"], sizes["tm"]),
        mesh=mesh,
        in_specs=(P("tm", "chan", None), P("chan", None), P("chan"), P("chan", None)),
        out_specs=P("chan", "tm", None, None, None),
        check_vma=False,
    )
```
